128 devices in a mesh: drift: 8 (over y, core), cross: 16 (over z, x).
Axes of the slice: x: 4, y: 4, z: 4, core: 2. Of those that a mesh axis runs over, the one named last changes fastest.
Arguments:
- points: float32 [16, 524288], P(None, ('drift', 'cross')), as said below
- send_counts: int32 [16384], P(('drift', 'cross')), may hold values from 1 to 32, as said below
- block_first: int32 [524288], P(('drift', 'cross')), may hold values from 0 to 63
- block_second: int32 [524288], P(('drift', 'cross')), may hold values from 0 to 63
- contact: float32 [524288], P(('drift', 'cross')), may hold values from 0 to 0.9
Outputs:
- final_points: float32 [16, 524288], P(None, ('drift', 'cross'))
- node_velocity: float32 [3, 524288], P(None, ('drift', 'cross'))
The draws below stay inside these ranges and needn't reach their ends.
Inputs may be any that keep to these rules, and one draw needn't show every extreme that they name: `send_counts`: every device's list of bounds holds the value 32 at least once. `points`: positions lie in 0.52 to 2.48 on every axis and masses are 0.49 or more.
All inputs are finite; a program needn't handle non-finite values.
Results may differ from the reference program's by a relative error of at most 0.0003.
Values sent between devices are 32-bit elements; how exact they have to be, the bound alone decides.
No kernel may reach another device: no remote copies, remote signals or barrier semaphores. Data moves between devices by JAX's collectives and lax.ppermute only.
A program may use at most 128 MiB of HBM per device.

```python
import jax
import jax.numpy as jnp
from jax import lax

CAP = 32
BLK_DEV = 64
MIG = 4
POINTS = 524288
BLOCKS = 8192
N_DRIFT = 8
N_CROSS = 16


def draw_points(key, part):
    key = jax.random.fold_in(key, 11)
    keys = jax.random.split(key, 4)
    count = POINTS
    position = jax.random.uniform(keys[0], (3, count), jnp.float32, 0.52, 2.48)
    velocity = jax.random.normal(keys[1], (3, count), jnp.float32)
    affine = 0.3 * jax.random.normal(keys[2], (9, count), jnp.float32)
    mass = jnp.exp(jax.random.uniform(keys[3], (1, count), jnp.float32, -0.7, 0.7))
    return jnp.concatenate([position, velocity, affine, mass], axis=0)


def draw_send_counts(key, part):
    key = jax.random.fold_in(key, 23)
    first, second = jax.random.split(key)
    devs = N_DRIFT * N_CROSS
    counts = jax.random.randint(first, (devs, devs), 1, CAP + 1)
    where = jax.random.randint(second, (devs,), 0, devs)
    column = jnp.arange(devs, dtype=jnp.int32)
    counts = jnp.where(column[None, :] == where[:, None], CAP, counts)
    return counts.reshape(-1).astype(jnp.int32)


def place_ends(drawn, own_key, low, top_value):
    dims = drawn.shape
    spot = [jax.random.randint(jax.random.fold_in(own_key, axis), (), 0, dims[axis]) for axis in range(len(dims))]
    drawn = drawn.at[tuple(spot)].set(low)
    longest = dims.index(max(dims))
    spot[longest] = (spot[longest] + 1) % dims[longest]
    return drawn.at[tuple(spot)].set(top_value)


def steps_of(own_key, dims, cuts, least, top_value):
    factor_of = 1.0
    for dim, blocks in cuts:
        heights = jax.random.uniform(jax.random.fold_in(jax.random.fold_in(own_key, 6), dim), (blocks,), jnp.float32, least / len(cuts), top_value / len(cuts))
        factor_of = factor_of * jnp.repeat(jnp.exp(heights), dims[dim] // blocks).reshape((-1,) + (1,) * (len(dims) - 1 - dim))
    return factor_of


def setup_inputs(seed: int = 0) -> dict:
    streams_of = jax.random.split(jax.random.key(seed), 6)
    return {
        "points": draw_points(jax.random.fold_in(streams_of[5], 71), 0),
        "send_counts": draw_send_counts(jax.random.fold_in(streams_of[5], 71), 0),
        "block_first": place_ends(jax.random.randint(streams_of[2], (POINTS,), 0, BLK_DEV), jax.random.fold_in(streams_of[2], 1), 0, BLK_DEV - 1).astype(jnp.int32),
        "block_second": place_ends(jax.random.randint(streams_of[3], (POINTS,), 0, BLK_DEV), jax.random.fold_in(streams_of[3], 1), 0, BLK_DEV - 1).astype(jnp.int32),
        "contact": jnp.clip(0.9 * jax.random.uniform(streams_of[4], (BLOCKS * 64,), jnp.float32) ** steps_of(streams_of[4], (BLOCKS * 64,), ((0, 128),), -0.2, 0.2), 0.0, 0.9),
    }


step_duration = 0.1
gravity_accel = 1.0


def spline(dist):
    size = jnp.abs(dist)
    near = 0.75 - size * size
    far = 0.5 * jnp.square(jnp.maximum(1.5 - size, 0.0))
    return jnp.where(size < 0.5, near, far)


def node_coords():
    index = jnp.arange(64, dtype=jnp.int32)
    return jnp.stack([index // 16, (index // 4) % 4, index % 4]).astype(jnp.float32)


def kernel_weights_for(position):
    nodes = jnp.arange(4, dtype=jnp.float32)
    first = spline(position[0][None, :] - nodes[:, None])
    second = spline(position[1][None, :] - nodes[:, None])
    third = spline(position[2][None, :] - nodes[:, None])
    full = first[:, None, None, :] * second[None, :, None, :] * third[None, None, :, :]
    return full.reshape(64, position.shape[1])


def contributions(state):
    position = state[0:3]
    velocity = state[3:6]
    affine = state[6:15].reshape(3, 3, -1)
    mass = state[15]
    weight = kernel_weights_for(position)
    offset = node_coords()[:, :, None] - position[:, None, :]
    moved = jnp.einsum('cer,enr->cnr', affine, offset, precision=lax.Precision.HIGHEST)
    momentum = weight[None] * mass[None, None, :] * (velocity[:, None, :] + moved)
    return jnp.concatenate([(weight * mass[None, :])[None], momentum], axis=0), weight, offset


def grid_update(scatter_totals, contact):
    grid_mass = jnp.maximum(scatter_totals[0], 0.5)
    velocity = scatter_totals[1:4] / grid_mass[None, :]
    velocity = velocity.at[2].add(-step_duration * gravity_accel)
    return velocity * (1.0 - contact)[None, :]


def gather_back(state, weight, offset, nodal):
    weighted = weight[None] * nodal
    velocity = jnp.sum(weighted, axis=1)
    affine = 4.0 * jnp.einsum('cnr,enr->cer', weighted, offset, precision=lax.Precision.HIGHEST)
    position = jnp.clip(state[0:3] + step_duration * velocity, 0.5, 2.5)
    stepped = jnp.concatenate([position, velocity, affine.reshape(9, -1), state[15:16]], axis=0)
    return jnp.where(state[15:16] > 0.0, stepped, state)


def one_step(state, global_ids, contact, devs):
    rows = state.shape[1] // devs
    pieces = state.reshape(16, devs, rows).transpose(1, 0, 2)
    id_pieces = global_ids.reshape(devs, rows)

    def add_source(total, item):
        piece, ids = item
        transfer_terms, weight, offset = contributions(piece)
        flat = transfer_terms.transpose(2, 0, 1)
        return total + jax.ops.segment_sum(flat, ids, num_segments=BLOCKS), None

    start = jnp.zeros((BLOCKS, 4, 64), jnp.float32)
    total, unused = lax.scan(add_source, start, (pieces, id_pieces))
    scatter_totals = total.transpose(1, 0, 2).reshape(4, BLOCKS * 64)
    velocity = grid_update(scatter_totals, contact)
    blocked = velocity.reshape(3, BLOCKS, 64)

    def back_source(item):
        piece, ids = item
        transfer_terms, weight, offset = contributions(piece)
        nodal = blocked[:, ids, :].transpose(0, 2, 1)
        return gather_back(piece, weight, offset, nodal)

    result = lax.map(back_source, (pieces, id_pieces))
    return result.transpose(1, 0, 2).reshape(16, -1), velocity


def reference(points, send_counts, block_first, block_second, contact):
    devs = N_DRIFT * N_CROSS
    slot = jnp.arange(CAP, dtype=jnp.int32)
    live = (slot[None, :] < send_counts[:, None]).astype(jnp.float32).reshape(-1)
    state = points.at[15].multiply(live)
    row = jnp.arange(POINTS, dtype=jnp.int32)
    owner = (row // CAP) % devs
    state, unused = one_step(state, owner * BLK_DEV + block_first, contact, devs)
    shaped = state.reshape(16, N_DRIFT, N_CROSS, devs, CAP)
    band_cross = jnp.roll(shaped[..., CAP - 2 * MIG:CAP - MIG], 1, axis=2)
    band_drift = jnp.roll(shaped[..., CAP - MIG:], 1, axis=1)
    shaped = jnp.concatenate([shaped[..., :CAP - 2 * MIG], band_cross, band_drift], axis=4)
    state = shaped.reshape(16, POINTS)
    state, velocity = one_step(state, owner * BLK_DEV + block_second, contact, devs)
    return state, velocity
```

```python
import jax
import jax.numpy as jnp
from jax import lax
from jax.experimental import pallas as pl
from jax.experimental.pallas import tpu as pltpu
from jax.sharding import PartitionSpec as P

CAP = 32
MIG = 4
NODES = 64
BLK_DEV = 64
DEVS = 128
N_CROSS = 16
LANES = 128

STEP_DURATION = 0.1
GRAVITY_ACCEL = 1.0

SEND_ROWS = 5
BACK_ROWS = 4

VMEM_LIMIT = 32 * 1024 * 1024


def spline(dist):
    size = jnp.abs(dist)
    near = 0.75 - size * size
    far = 0.5 * jnp.square(jnp.maximum(1.5 - size, 0.0))
    return jnp.where(size < 0.5, near, far)


def pack_kernel(points_ref, counts_ref, first_ref, second_ref, out_ref, counts_col):
    counts = counts_ref[...].astype(jnp.float32)
    counts_col[...] = jnp.broadcast_to(counts, (DEVS, LANES)).T
    lane = lax.broadcasted_iota(jnp.int32, (32, LANES), 1)
    part = lane // CAP

    def feature(f):
        if f < 16:
            return points_ref[f // 8, :, f % 8, :]
        return (first_ref if f == 16 else second_ref)[...].astype(jnp.float32)

    for j in range(SEND_ROWS):
        rows = [feature(4 * j + ff) for ff in range(4) if 4 * j + ff < 18]
        for oo in range(4):
            block = jnp.zeros((32, LANES), jnp.float32)
            for ff, row in enumerate(rows):
                moved = pltpu.roll(row, ((ff - oo) * CAP) % LANES, 1) if ff != oo else row
                block = jnp.where(part == ff, moved, block)
            if j == 3:
                count = counts_col[pl.ds(oo, 32, stride=4), :]
                slot = (lane - 3 * CAP).astype(jnp.float32)
                live = (slot < count).astype(jnp.float32)
                block = jnp.where(part == 3, block * live, block)
            out_ref[pl.ds(SEND_ROWS * oo + j, 32, stride=4 * SEND_ROWS), :] = block


def unpack_kernel(back_ref, out_ref):
    lane = lax.broadcasted_iota(jnp.int32, (32, LANES), 1)
    part = lane // CAP
    for j in range(BACK_ROWS):
        blocks = [back_ref[pl.ds(BACK_ROWS * oo + j, 32, stride=4 * BACK_ROWS), :] for oo in range(4)]
        for ff in range(4):
            f = 4 * j + ff
            row = blocks[0]
            for oo, block in enumerate(blocks):
                moved = pltpu.roll(block, ((oo - ff) * CAP) % LANES, 1) if ff != oo else block
                row = jnp.where(part == oo, moved, row)
            out_ref[f // 8, :, f % 8, :] = row


def steps_kernel(
    got_ref, contact_ref, back_ref, vel_ref, state, terms, patterns, sums, selector, parts, reduced, keep, pairs
):
    def rows_of(f):
        return state[f * CAP : (f + 1) * CAP, :]

    def put(f, value):
        state[f * CAP : (f + 1) * CAP, :] = value

    for j in range(SEND_ROWS):
        state[j * LANES : (j + 1) * LANES, :] = got_ref[pl.ds(j, DEVS, stride=SEND_ROWS), :].T

    contact = contact_ref[...]
    pairs[pl.ds(0, 32, stride=2), :] = contact
    pairs[pl.ds(1, 32, stride=2), :] = pltpu.roll(contact, NODES, 1)
    turned = jnp.concatenate([pairs[...], pairs[...]], axis=0).T
    keep[...] = 1.0 - turned[0:NODES, :]

    sub = lax.broadcasted_iota(jnp.int32, (8, LANES), 0)
    k_of = (sub % 4).astype(jnp.float32)
    j_of = (sub // 4).astype(jnp.float32)
    block_of = lax.broadcasted_iota(jnp.int32, (BLK_DEV, LANES), 0).astype(jnp.float32)
    half = lax.broadcasted_iota(jnp.int32, (3 * NODES, LANES), 1) < BLK_DEV

    def one_step(ids_row):
        position = [rows_of(e) for e in range(3)]
        velocity = [rows_of(3 + c) for c in range(3)]
        affine = [[rows_of(6 + 3 * c + e) for e in range(3)] for c in range(3)]
        mass = rows_of(15)

        def put_term(q, value):
            terms[q * CAP : (q + 1) * CAP, :] = value

        put_term(0, mass)
        for c in range(3):
            moved = affine[c][0] * position[0] + affine[c][1] * position[1] + affine[c][2] * position[2]
            put_term(1 + c, velocity[c] - moved)
            for e in range(3):
                put_term(4 + 3 * c + e, affine[c][e])
        for i in range(4):
            put_term(13 + i, spline(position[0] - float(i)))
        middle = [spline(position[1] - float(i)) for i in range(4)]
        last = [spline(position[2] - float(i)) for i in range(4)]
        for r in range(8):
            patterns[r * CAP : (r + 1) * CAP, :] = last[r % 4]
            patterns[(8 + r) * CAP : (9 + r) * CAP, :] = middle[r // 4]
            patterns[(16 + r) * CAP : (17 + r) * CAP, :] = middle[2 + r // 4]

        def term(q, c):
            return terms[pl.ds(q * CAP + c, 1), :]

        def pair_weights(c):
            third = patterns[pl.ds(c, 8, stride=CAP), :]
            return [patterns[pl.ds(8 * (1 + h) * CAP + c, 8, stride=CAP), :] * third for h in range(2)]

        sums[...] = jnp.zeros_like(sums)

        def scatter(c, unused):
            ids = state[pl.ds(ids_row * CAP + c, 1), :]
            chosen = jnp.where(block_of == ids, 1.0, 0.0).astype(jnp.bfloat16)
            selector[c] = chosen
            inner = [w * term(0, c) for w in pair_weights(c)]
            weights = [term(13 + i, c) * inner[h] for i in range(4) for h in range(2)]
            pieces = list(weights)
            for v in range(3):
                along = term(4 + 3 * v, c)
                start = term(1 + v, c) + term(6 + 3 * v, c) * k_of
                middle_term = term(5 + 3 * v, c)
                at = [start + middle_term * j_of, start + middle_term * (j_of + 2.0)]
                for i in range(4):
                    for h in range(2):
                        pieces.append(weights[2 * i + h] * at[h])
                    at = [a + along for a in at]
            full = jnp.concatenate(pieces, axis=0)
            high = full.astype(jnp.bfloat16)
            low = (full - high.astype(jnp.float32)).astype(jnp.bfloat16)
            twice = jnp.concatenate([chosen, chosen], axis=0)
            sums[...] += lax.dot_general(
                jnp.concatenate([high, low], axis=1),
                jnp.concatenate([twice, twice], axis=1),
                (((1,), (1,)), ((), ())),
                preferred_element_type=jnp.float32,
            )
            return unused

        lax.fori_loop(0, CAP, scatter, 0)

        grid_mass = jnp.maximum(sums[0:NODES, :], 0.5)
        node = []
        for v in range(3):
            value = sums[(1 + v) * NODES : (2 + v) * NODES, :] / grid_mass
            if v == 2:
                value = value - STEP_DURATION * GRAVITY_ACCEL
            node.append(value * keep[...])
        whole = jnp.concatenate(node, axis=0)
        first = whole.astype(jnp.bfloat16).astype(jnp.float32)
        rest = whole - first
        second = rest.astype(jnp.bfloat16).astype(jnp.float32)
        third = jnp.where(half, rest - second, 0.0)
        parts[:, 0:LANES] = jnp.where(half, first, second).astype(jnp.bfloat16)
        parts[:, LANES : 2 * LANES] = third.astype(jnp.bfloat16)

        def gather(c, unused):
            chosen = selector[c]
            nodal = jnp.dot(
                parts[...],
                jnp.concatenate([chosen, chosen, chosen, chosen], axis=0),
                preferred_element_type=jnp.float32,
            )
            inner = pair_weights(c)
            weights = [term(13 + i, c) * inner[h] for i in range(4) for h in range(2)]
            for v in range(3):
                weighted = [
                    weights[n] * nodal[v * NODES + 8 * n : v * NODES + 8 * (n + 1), :] for n in range(8)
                ]
                by_i = [weighted[2 * i] + weighted[2 * i + 1] for i in range(4)]
                odd = (weighted[1] + weighted[3]) + (weighted[5] + weighted[7])
                outer = by_i[2] + by_i[3]
                total = (by_i[0] + by_i[1]) + outer
                first_moment = (by_i[1] + by_i[3]) + (outer + outer)
                for t, value in enumerate((total, odd, first_moment)):
                    reduced[pl.ds((3 * v + t) * 8 * CAP + c * 8, 8), :] = value
            return unused

        lax.fori_loop(0, CAP, gather, 0)

        def spread(v, t):
            return [reduced[pl.ds((3 * v + t) * 8 * CAP + r, CAP, stride=8), :] for r in range(8)]

        def add_all(values):
            total = values[0]
            for value in values[1:]:
                total = total + value
            return total

        alive = mass > 0.0
        for v in range(3):
            by_row = spread(v, 0)
            by_k = [by_row[k] + by_row[4 + k] for k in range(4)]
            new_velocity = (by_k[0] + by_k[1]) + (by_k[2] + by_k[3])
            moment = [
                add_all(spread(v, 2)),
                2.0 * add_all(spread(v, 1)) + add_all(by_row[4:]),
                (by_k[1] + by_k[3]) + 2.0 * (by_k[2] + by_k[3]),
            ]
            for e in range(3):
                new_affine = 4.0 * (moment[e] - position[e] * new_velocity)
                put(6 + 3 * v + e, jnp.where(alive, new_affine, affine[v][e]))
            put(3 + v, jnp.where(alive, new_velocity, velocity[v]))
            new_position = jnp.clip(position[v] + STEP_DURATION * new_velocity, 0.5, 2.5)
            put(v, jnp.where(alive, new_position, position[v]))
        return node

    one_step(16)

    source = lax.broadcasted_iota(jnp.int32, (2 * MIG, LANES), 1)
    slot = lax.broadcasted_iota(jnp.int32, (2 * MIG, LANES), 0)
    for f in range(16):
        at = f * CAP + CAP - 2 * MIG
        old = state[at : at + 2 * MIG, :]
        across = jnp.where(
            source % N_CROSS == 0, pltpu.roll(old, LANES - (N_CROSS - 1), 1), pltpu.roll(old, 1, 1)
        )
        state[at : at + 2 * MIG, :] = jnp.where(slot < MIG, across, pltpu.roll(old, N_CROSS, 1))

    node = one_step(17)

    for j in range(BACK_ROWS):
        back_ref[pl.ds(j, DEVS, stride=BACK_ROWS), :] = state[j * LANES : (j + 1) * LANES, :].T

    lane = lax.broadcasted_iota(jnp.int32, (32, LANES), 1)
    for v in range(3):
        pairs[...] = jnp.concatenate([node[v], node[v]], axis=0).T[0:BLK_DEV, :]
        packed = jnp.where(lane < NODES, pairs[pl.ds(0, 32, stride=2), :], pairs[pl.ds(1, 32, stride=2), :])
        for q in range(32):
            vel_ref[v : v + 1, q * LANES : (q + 1) * LANES] = packed[q : q + 1, :]


def in_vmem(count):
    return [pl.BlockSpec(memory_space=pltpu.VMEM)] * count


def local(points, send_counts, block_first, block_second, contact):
    params = pltpu.CompilerParams(vmem_limit_bytes=VMEM_LIMIT)
    tiled = points.reshape(2, 8, 32, LANES).transpose(0, 2, 1, 3)
    send = pl.pallas_call(
        pack_kernel,
        out_shape=jax.ShapeDtypeStruct((DEVS * SEND_ROWS, LANES), jnp.float32),
        in_specs=in_vmem(4),
        out_specs=in_vmem(1)[0],
        scratch_shapes=[pltpu.VMEM((DEVS, LANES), jnp.float32)],
        compiler_params=params,
    )(tiled, send_counts.reshape(1, DEVS), block_first.reshape(32, LANES), block_second.reshape(32, LANES))
    got = lax.all_to_all(
        send.reshape(DEVS, 1, SEND_ROWS * LANES), ("drift", "cross"), split_axis=0, concat_axis=0, tiled=True
    )
    back, node_velocity = pl.pallas_call(
        steps_kernel,
        out_shape=(
            jax.ShapeDtypeStruct((DEVS * BACK_ROWS, LANES), jnp.float32),
            jax.ShapeDtypeStruct((3, BLK_DEV * NODES), jnp.float32),
        ),
        in_specs=in_vmem(2),
        out_specs=tuple(in_vmem(2)),
        scratch_shapes=[
            pltpu.VMEM((SEND_ROWS * LANES, LANES), jnp.float32),
            pltpu.VMEM((17 * CAP, LANES), jnp.float32),
            pltpu.VMEM((24 * CAP, LANES), jnp.float32),
            pltpu.VMEM((4 * NODES, LANES), jnp.float32),
            pltpu.VMEM((CAP, BLK_DEV, LANES), jnp.bfloat16),
            pltpu.VMEM((3 * NODES, 2 * LANES), jnp.bfloat16),
            pltpu.VMEM((9 * 8 * CAP, LANES), jnp.float32),
            pltpu.VMEM((NODES, LANES), jnp.float32),
            pltpu.VMEM((BLK_DEV, LANES), jnp.float32),
        ],
        compiler_params=params,
    )(got.reshape(DEVS * SEND_ROWS, LANES), contact.reshape(32, LANES))
    returned = lax.all_to_all(
        back.reshape(DEVS, 1, BACK_ROWS * LANES), ("drift", "cross"), split_axis=0, concat_axis=0, tiled=True
    )
    final = pl.pallas_call(
        unpack_kernel,
        out_shape=jax.ShapeDtypeStruct((2, 32, 8, LANES), jnp.float32),
        in_specs=in_vmem(1),
        out_specs=in_vmem(1)[0],
        compiler_params=params,
    )(returned.reshape(DEVS * BACK_ROWS, LANES))
    return (final.transpose(0, 2, 1, 3).reshape(16, DEVS * CAP), node_velocity)


def solution(mesh):
    return jax.shard_map(
        local,
        mesh=mesh,
        in_specs=(
            P(None, ("drift", "cross")),
            P(("drift", "cross")),
            P(("drift", "cross")),
            P(("drift", "cross")),
            P(("drift", "cross")),
        ),
        out_specs=(P(None, ("drift", "cross")), P(None, ("drift", "cross"))),
        check_vma=False,
    )
```

```python
import jax
import jax.numpy as jnp
from jax import lax
from jax.experimental import pallas as pl
from jax.experimental.pallas import tpu as pltpu
from jax.sharding import PartitionSpec as P

CAP = 32
MIG = 4
GROUP = 8
NODES = 64
BLK_DEV = 64
DEVS = 128
N_CROSS = 16
LANES = 128

STEP_DURATION = 0.1
GRAVITY_ACCEL = 1.0

SEND_ROWS = 5
BACK_ROWS = 4

VMEM_LIMIT = 32 * 1024 * 1024


def spline(dist):
    size = jnp.abs(dist)
    near = 0.75 - size * size
    far = 0.5 * jnp.square(jnp.maximum(1.5 - size, 0.0))
    return jnp.where(size < 0.5, near, far)


def pack_kernel(
    points_hbm, counts_hbm, first_hbm, second_hbm, out_ref, points_ref, counts_ref, first_ref, second_ref, counts_col, sems
):
    copies = [
        pltpu.make_async_copy(counts_hbm, counts_ref, sems.at[0]),
        pltpu.make_async_copy(points_hbm.at[0], points_ref.at[0], sems.at[1]),
        pltpu.make_async_copy(points_hbm.at[1], points_ref.at[1], sems.at[2]),
        pltpu.make_async_copy(first_hbm, first_ref, sems.at[3]),
        pltpu.make_async_copy(second_hbm, second_ref, sems.at[4]),
    ]
    for copy in copies:
        copy.start()
    lane = lax.broadcasted_iota(jnp.int32, (32, LANES), 1)
    part = lane // CAP
    copies[0].wait()
    counts = counts_ref[...].astype(jnp.float32)
    counts_col[...] = jnp.broadcast_to(counts, (DEVS, LANES)).T

    def feature(f):
        if f < 16:
            return points_ref[f // 8, :, f % 8, :]
        return (first_ref if f == 16 else second_ref)[...].astype(jnp.float32)

    for j in range(SEND_ROWS):
        if j % 2 == 0:
            copies[1 + j // 2].wait()
        if j == 4:
            copies[4].wait()
        rows = [feature(4 * j + ff) for ff in range(4) if 4 * j + ff < 18]
        for oo in range(4):
            block = jnp.zeros((32, LANES), jnp.float32)
            for ff, row in enumerate(rows):
                moved = pltpu.roll(row, ((ff - oo) * CAP) % LANES, 1) if ff != oo else row
                block = jnp.where(part == ff, moved, block)
            if j == 3:
                count = counts_col[pl.ds(oo, 32, stride=4), :]
                slot = (lane - 3 * CAP).astype(jnp.float32)
                live = (slot < count).astype(jnp.float32)
                block = jnp.where(part == 3, block * live, block)
            out_ref[pl.ds(SEND_ROWS * oo + j, 32, stride=4 * SEND_ROWS), :] = block


def unpack_kernel(back_ref, out_hbm, out_ref, sems):
    lane = lax.broadcasted_iota(jnp.int32, (32, LANES), 1)
    part = lane // CAP
    copies = [pltpu.make_async_copy(out_ref.at[a], out_hbm.at[a], sems.at[a]) for a in range(2)]
    for j in range(BACK_ROWS):
        blocks = [back_ref[pl.ds(BACK_ROWS * oo + j, 32, stride=4 * BACK_ROWS), :] for oo in range(4)]
        for ff in range(4):
            f = 4 * j + ff
            row = blocks[0]
            for oo, block in enumerate(blocks):
                moved = pltpu.roll(block, ((oo - ff) * CAP) % LANES, 1) if ff != oo else block
                row = jnp.where(part == oo, moved, row)
            out_ref[f // 8, :, f % 8, :] = row
        if j % 2 == 1:
            copies[j // 2].start()
    for copy in copies:
        copy.wait()


def steps_kernel(
    got_ref, contact_ref, back_ref, vel_hbm, state, terms, patterns, sums, selector, parts, reduced, keep, pairs, vel, sem
):
    def rows_of(f):
        return state[f * CAP : (f + 1) * CAP, :]

    def put(f, value):
        state[f * CAP : (f + 1) * CAP, :] = value

    for j in range(SEND_ROWS):
        state[j * LANES : (j + 1) * LANES, :] = got_ref[pl.ds(j, DEVS, stride=SEND_ROWS), :].T

    contact = contact_ref[...]
    pairs[pl.ds(0, 32, stride=2), :] = contact
    pairs[pl.ds(1, 32, stride=2), :] = pltpu.roll(contact, NODES, 1)
    turned = jnp.concatenate([pairs[...], pairs[...]], axis=0).T
    keep[...] = 1.0 - turned[0:NODES, :]

    sub = lax.broadcasted_iota(jnp.int32, (8, LANES), 0)
    k_of = (sub % 4).astype(jnp.float32)
    j_of = (sub // 4).astype(jnp.float32)
    block_of = lax.broadcasted_iota(jnp.int32, (BLK_DEV, LANES), 0).astype(jnp.float32)
    half = lax.broadcasted_iota(jnp.int32, (3 * NODES, LANES), 1) < BLK_DEV

    def one_step(ids_row, when_node=None):
        position = [rows_of(e) for e in range(3)]
        velocity = [rows_of(3 + c) for c in range(3)]
        affine = [[rows_of(6 + 3 * c + e) for e in range(3)] for c in range(3)]
        mass = rows_of(15)

        def put_term(q, value):
            terms[q * CAP : (q + 1) * CAP, :] = value

        put_term(0, mass)
        for c in range(3):
            moved = affine[c][0] * position[0] + affine[c][1] * position[1] + affine[c][2] * position[2]
            put_term(1 + c, velocity[c] - moved)
            for e in range(3):
                put_term(4 + 3 * c + e, affine[c][e])
        for i in range(4):
            put_term(13 + i, spline(position[0] - float(i)))
        middle = [spline(position[1] - float(i)) for i in range(4)]
        last = [spline(position[2] - float(i)) for i in range(4)]
        for r in range(8):
            patterns[r * CAP : (r + 1) * CAP, :] = last[r % 4]
            patterns[(8 + r) * CAP : (9 + r) * CAP, :] = middle[r // 4]
            patterns[(16 + r) * CAP : (17 + r) * CAP, :] = middle[2 + r // 4]

        def term(q, c):
            return terms[pl.ds(q * CAP + c, 1), :]

        def pair_weights(c):
            third = patterns[pl.ds(c, 8, stride=CAP), :]
            return [patterns[pl.ds(8 * (1 + h) * CAP + c, 8, stride=CAP), :] * third for h in range(2)]

        sums[...] = jnp.zeros_like(sums)

        def scatter_operands(c):
            ids = state[pl.ds(ids_row * CAP + c, 1), :]
            chosen = jnp.where(block_of == ids, 1.0, 0.0).astype(jnp.bfloat16)
            selector[c] = chosen
            inner = [w * term(0, c) for w in pair_weights(c)]
            weights = [term(13 + i, c) * inner[h] for i in range(4) for h in range(2)]
            pieces = list(weights)
            for v in range(3):
                along = term(4 + 3 * v, c)
                start = term(1 + v, c) + term(6 + 3 * v, c) * k_of
                middle_term = term(5 + 3 * v, c)
                at = [start + middle_term * j_of, start + middle_term * (j_of + 2.0)]
                for i in range(4):
                    for h in range(2):
                        pieces.append(weights[2 * i + h] * at[h])
                    at = [a + along for a in at]
            full = jnp.concatenate(pieces, axis=0)
            high = full.astype(jnp.bfloat16)
            low = (full - high.astype(jnp.float32)).astype(jnp.bfloat16)
            twice = jnp.concatenate([chosen, chosen], axis=0)
            return [high, low], [twice, twice]

        def scatter(step, unused):
            values, selectors = [], []
            for u in range(GROUP):
                a, b = scatter_operands(GROUP * step + u)
                values += a
                selectors += b
            sums[...] += lax.dot_general(
                jnp.concatenate(values, axis=1),
                jnp.concatenate(selectors, axis=1),
                (((1,), (1,)), ((), ())),
                preferred_element_type=jnp.float32,
            )
            return unused

        lax.fori_loop(0, CAP // GROUP, scatter, 0, unroll=2)

        grid_mass = jnp.maximum(sums[0:NODES, :], 0.5)
        node = []
        for v in range(3):
            value = sums[(1 + v) * NODES : (2 + v) * NODES, :] / grid_mass
            if v == 2:
                value = value - STEP_DURATION * GRAVITY_ACCEL
            node.append(value * keep[...])
        if when_node is not None:
            when_node(node)
        whole = jnp.concatenate(node, axis=0)
        first = whole.astype(jnp.bfloat16).astype(jnp.float32)
        rest = whole - first
        second = rest.astype(jnp.bfloat16).astype(jnp.float32)
        third = jnp.where(half, rest - second, 0.0)
        parts[:, 0:LANES] = jnp.where(half, first, second).astype(jnp.bfloat16)
        parts[:, LANES : 2 * LANES] = third.astype(jnp.bfloat16)

        def gather(step, unused):
            chosen = jnp.concatenate([selector[GROUP * step + u] for u in range(GROUP)], axis=1)
            nodal_all = jnp.dot(
                parts[...],
                jnp.concatenate([chosen, chosen, chosen, chosen], axis=0),
                preferred_element_type=jnp.float32,
            )
            for u in range(GROUP):
                c = GROUP * step + u
                nodal = nodal_all[:, u * LANES : (u + 1) * LANES]
                inner = pair_weights(c)
                weights = [term(13 + i, c) * inner[h] for i in range(4) for h in range(2)]
                for v in range(3):
                    weighted = [
                        weights[n] * nodal[v * NODES + 8 * n : v * NODES + 8 * (n + 1), :] for n in range(8)
                    ]
                    by_i = [weighted[2 * i] + weighted[2 * i + 1] for i in range(4)]
                    odd = (weighted[1] + weighted[3]) + (weighted[5] + weighted[7])
                    outer = by_i[2] + by_i[3]
                    total = (by_i[0] + by_i[1]) + outer
                    first_moment = (by_i[1] + by_i[3]) + (outer + outer)
                    for t, value in enumerate((total, odd, first_moment)):
                        reduced[pl.ds((3 * v + t) * 8 * CAP + c * 8, 8), :] = value
            return unused

        lax.fori_loop(0, CAP // GROUP, gather, 0, unroll=2)

        def spread(v, t):
            return [reduced[pl.ds((3 * v + t) * 8 * CAP + r, CAP, stride=8), :] for r in range(8)]

        def add_all(values):
            total = values[0]
            for value in values[1:]:
                total = total + value
            return total

        alive = mass > 0.0
        for v in range(3):
            by_row = spread(v, 0)
            by_k = [by_row[k] + by_row[4 + k] for k in range(4)]
            new_velocity = (by_k[0] + by_k[1]) + (by_k[2] + by_k[3])
            moment = [
                add_all(spread(v, 2)),
                2.0 * add_all(spread(v, 1)) + add_all(by_row[4:]),
                (by_k[1] + by_k[3]) + 2.0 * (by_k[2] + by_k[3]),
            ]
            for e in range(3):
                new_affine = 4.0 * (moment[e] - position[e] * new_velocity)
                put(6 + 3 * v + e, jnp.where(alive, new_affine, affine[v][e]))
            put(3 + v, jnp.where(alive, new_velocity, velocity[v]))
            new_position = jnp.clip(position[v] + STEP_DURATION * new_velocity, 0.5, 2.5)
            put(v, jnp.where(alive, new_position, position[v]))

    one_step(16)

    source = lax.broadcasted_iota(jnp.int32, (2 * MIG, LANES), 1)
    slot = lax.broadcasted_iota(jnp.int32, (2 * MIG, LANES), 0)
    for f in range(16):
        at = f * CAP + CAP - 2 * MIG
        old = state[at : at + 2 * MIG, :]
        across = jnp.where(
            source % N_CROSS == 0, pltpu.roll(old, LANES - (N_CROSS - 1), 1), pltpu.roll(old, 1, 1)
        )
        state[at : at + 2 * MIG, :] = jnp.where(slot < MIG, across, pltpu.roll(old, N_CROSS, 1))

    copy = pltpu.make_async_copy(vel, vel_hbm, sem)

    def send_velocity(node):
        lane = lax.broadcasted_iota(jnp.int32, (32, LANES), 1)
        for v in range(3):
            pairs[...] = jnp.concatenate([node[v], node[v]], axis=0).T[0:BLK_DEV, :]
            packed = jnp.where(lane < NODES, pairs[pl.ds(0, 32, stride=2), :], pairs[pl.ds(1, 32, stride=2), :])
            for q in range(32):
                vel[v : v + 1, q * LANES : (q + 1) * LANES] = packed[q : q + 1, :]
        copy.start()

    one_step(17, send_velocity)

    for j in range(BACK_ROWS):
        back_ref[pl.ds(j, DEVS, stride=BACK_ROWS), :] = state[j * LANES : (j + 1) * LANES, :].T

    copy.wait()


def in_vmem(count):
    return [pl.BlockSpec(memory_space=pltpu.VMEM)] * count


def in_hbm(count):
    return [pl.BlockSpec(memory_space=pltpu.HBM)] * count


def local(points, send_counts, block_first, block_second, contact):
    params = pltpu.CompilerParams(vmem_limit_bytes=VMEM_LIMIT)
    tiled = points.reshape(2, 8, 32, LANES).transpose(0, 2, 1, 3)
    operands = (tiled, send_counts.reshape(1, DEVS), block_first.reshape(32, LANES), block_second.reshape(32, LANES))
    send = pl.pallas_call(
        pack_kernel,
        out_shape=jax.ShapeDtypeStruct((DEVS * SEND_ROWS, LANES), jnp.float32),
        in_specs=in_hbm(4),
        out_specs=in_vmem(1)[0],
        scratch_shapes=[
            pltpu.VMEM((2, 32, 8, LANES), jnp.float32),
            pltpu.VMEM((1, DEVS), jnp.int32),
            pltpu.VMEM((32, LANES), jnp.int32),
            pltpu.VMEM((32, LANES), jnp.int32),
            pltpu.VMEM((DEVS, LANES), jnp.float32),
            pltpu.SemaphoreType.DMA((5,)),
        ],
        compiler_params=params,
    )(*(pltpu.with_memory_space_constraint(value, pltpu.HBM) for value in operands))
    got = lax.all_to_all(
        send.reshape(DEVS, 1, SEND_ROWS * LANES), ("drift", "cross"), split_axis=0, concat_axis=0, tiled=True
    )
    back, node_velocity = pl.pallas_call(
        steps_kernel,
        out_shape=(
            jax.ShapeDtypeStruct((DEVS * BACK_ROWS, LANES), jnp.float32),
            jax.ShapeDtypeStruct((3, BLK_DEV * NODES), jnp.float32),
        ),
        in_specs=in_vmem(2),
        out_specs=(in_vmem(1)[0], in_hbm(1)[0]),
        scratch_shapes=[
            pltpu.VMEM((SEND_ROWS * LANES, LANES), jnp.float32),
            pltpu.VMEM((17 * CAP, LANES), jnp.float32),
            pltpu.VMEM((24 * CAP, LANES), jnp.float32),
            pltpu.VMEM((4 * NODES, LANES), jnp.float32),
            pltpu.VMEM((CAP, BLK_DEV, LANES), jnp.bfloat16),
            pltpu.VMEM((3 * NODES, 2 * LANES), jnp.bfloat16),
            pltpu.VMEM((9 * 8 * CAP, LANES), jnp.float32),
            pltpu.VMEM((NODES, LANES), jnp.float32),
            pltpu.VMEM((BLK_DEV, LANES), jnp.float32),
            pltpu.VMEM((3, BLK_DEV * NODES), jnp.float32),
            pltpu.SemaphoreType.DMA(()),
        ],
        compiler_params=params,
    )(got.reshape(DEVS * SEND_ROWS, LANES), contact.reshape(32, LANES))
    returned = lax.all_to_all(
        back.reshape(DEVS, 1, BACK_ROWS * LANES), ("drift", "cross"), split_axis=0, concat_axis=0, tiled=True
    )
    final = pl.pallas_call(
        unpack_kernel,
        out_shape=jax.ShapeDtypeStruct((2, 32, 8, LANES), jnp.float32),
        in_specs=in_vmem(1),
        out_specs=in_hbm(1)[0],
        scratch_shapes=[pltpu.VMEM((2, 32, 8, LANES), jnp.float32), pltpu.SemaphoreType.DMA((2,))],
        compiler_params=params,
    )(returned.reshape(DEVS * BACK_ROWS, LANES))
    return (final.transpose(0, 2, 1, 3).reshape(16, DEVS * CAP), node_velocity)


def solution(mesh):
    return jax.shard_map(
        local,
        mesh=mesh,
        in_specs=(
            P(None, ("drift", "cross")),
            P(("drift", "cross")),
            P(("drift", "cross")),
            P(("drift", "cross")),
            P(("drift", "cross")),
        ),
        out_specs=(P(None, ("drift", "cross")), P(None, ("drift", "cross"))),
        check_vma=False,
    )
```

```python
import jax
import jax.numpy as jnp
from jax import lax
from jax.experimental import pallas as pl
from jax.experimental.pallas import tpu as pltpu
from jax.sharding import PartitionSpec as P

CAP = 32
MIG = 4
NODES = 64
BLK_DEV = 64
DEVS = 128
N_CROSS = 16
LANES = 128

STEP_DURATION = 0.1
GRAVITY_ACCEL = 1.0

SEND_ROWS = 5
BACK_ROWS = 4

UNPACK_PARTS = 2

ROW = 23
SLOT = 3

VMEM_LIMIT = 32 * 1024 * 1024


def spline(dist):
    size = jnp.abs(dist)
    near = 0.75 - size * size
    far = 0.5 * jnp.square(jnp.maximum(1.5 - size, 0.0))
    return jnp.where(size < 0.5, near, far)


def pack_kernel(
    points_hbm, counts_hbm, first_hbm, second_hbm, out_ref, points_ref, counts_ref, first_ref, second_ref, counts_col, sems
):
    moves = ((counts_hbm, counts_ref), (points_hbm, points_ref), (first_hbm, first_ref), (second_hbm, second_ref))
    copies = [pltpu.make_async_copy(source, target, sems.at[n]) for n, (source, target) in enumerate(moves)]
    for copy in copies:
        copy.start()
    lane = lax.broadcasted_iota(jnp.int32, (32, LANES), 1)
    quarter = lane // CAP
    slot = (lane - 3 * CAP).astype(jnp.float32)
    copies[0].wait()
    counts = counts_ref[...].astype(jnp.float32)
    counts_col[...] = jnp.broadcast_to(counts, (DEVS, LANES)).T
    for copy in copies[1:]:
        copy.wait()

    def feature(f):
        if f < 16:
            return points_ref[f // 8, :, f % 8, :]
        return (first_ref if f == 16 else second_ref)[...].astype(jnp.float32)

    for j in range(SEND_ROWS):
        rows = [feature(4 * j + ff) for ff in range(4) if 4 * j + ff < 18]
        for oo in range(4):
            block = jnp.zeros((32, LANES), jnp.float32)
            for ff, row in enumerate(rows):
                moved = pltpu.roll(row, ((ff - oo) * CAP) % LANES, 1) if ff != oo else row
                block = jnp.where(quarter == ff, moved, block)
            if j == 3:
                count = counts_col[pl.ds(oo, 32, stride=4), :]
                live = (slot < count).astype(jnp.float32)
                block = jnp.where(quarter == 3, block * live, block)
            out_ref[pl.ds(SEND_ROWS * oo + j, 32, stride=4 * SEND_ROWS), :] = block


def unpack_kernel(back_ref, out_hbm, out_ref, sems):
    tiles = 32 // UNPACK_PARTS
    lane = lax.broadcasted_iota(jnp.int32, (tiles, LANES), 1)
    quarter = lane // CAP
    copies = []
    for part in range(UNPACK_PARTS):
        at = slice(tiles * part, tiles * (part + 1))
        for j in range(BACK_ROWS):
            from_row = 4 * BACK_ROWS * tiles * part + j
            blocks = [back_ref[pl.ds(from_row + BACK_ROWS * oo, tiles, stride=4 * BACK_ROWS), :] for oo in range(4)]
            for ff in range(4):
                f = 4 * j + ff
                row = blocks[0]
                for oo, block in enumerate(blocks):
                    moved = pltpu.roll(block, ((oo - ff) * CAP) % LANES, 1) if ff != oo else block
                    row = jnp.where(quarter == oo, moved, row)
                out_ref[f // 8, at, f % 8, :] = row
        piece = pl.ds(tiles * part, tiles)
        copies.append(pltpu.make_async_copy(out_ref.at[:, piece], out_hbm.at[:, piece], sems.at[part]))
        copies[-1].start()
    for copy in copies:
        copy.wait()


def steps_kernel(
    got_ref,
    contact_ref,
    back_ref,
    vel_hbm,
    state,
    cells,
    values,
    weights,
    sums,
    nodes,
    parts,
    reduced,
    keep,
    pairs,
    vel,
    sem,
):
    def rows_of(f):
        return state[f * CAP : (f + 1) * CAP, :]

    def put(f, value):
        state[f * CAP : (f + 1) * CAP, :] = value

    for j in range(SEND_ROWS):
        state[j * LANES : (j + 1) * LANES, :] = got_ref[pl.ds(j, DEVS, stride=SEND_ROWS), :].T

    contact = contact_ref[...]
    pairs[pl.ds(0, 32, stride=2), :] = contact
    pairs[pl.ds(1, 32, stride=2), :] = pltpu.roll(contact, NODES, 1)
    turned = jnp.concatenate([pairs[...], pairs[...]], axis=0).T
    keep[...] = 1.0 - turned[0:NODES, :]

    def half(rows):
        return lax.broadcasted_iota(jnp.int32, (rows, LANES), 1) < BLK_DEV

    def numbers(rows):
        return lax.broadcasted_iota(jnp.int32, (rows, LANES), 0).astype(jnp.float32)

    def chosen(row, rows):
        return jnp.where(numbers(rows) == row, 1.0, 0.0).astype(jnp.bfloat16)

    sub = lax.broadcasted_iota(jnp.int32, (8, LANES), 0)
    k_of = (sub % 4).astype(jnp.float32)
    j_of = (sub // 4).astype(jnp.float32)

    def one_step(ids_row, when_node=None):
        sums[...] = jnp.zeros_like(sums)

        def scatter(group, unused):
            def feature(f):
                return state[pl.ds(pl.multiple_of(f * CAP + 8 * group, 8), 8), :]

            position = [feature(e) for e in range(3)]
            mass = feature(15)
            cell = jnp.where(position[0] >= 1.5, 1.0, 0.0)
            within = position[0] - cell
            at_cells = pl.ds(pl.multiple_of(8 * group, 8), 8)
            cells[at_cells, :] = feature(ids_row) + BLK_DEV * cell
            first = [spline(within - float(o)) for o in range(3)]
            second = [spline(position[1] - float(j)) for j in range(4)]
            third = [spline(position[2] - float(k)) for k in range(4)]
            for o in range(3):
                for j in range(4):
                    product = first[o] * second[j]
                    for k in range(4):
                        r = 16 * o + 4 * j + k
                        weights[group, pl.ds(ROW * r, 8, stride=SLOT), :] = product * third[k]

            def write(q, value):
                values[group, 8 * q : 8 * q + 8, :] = value

            write(0, mass)
            for v in range(3):
                along = [feature(6 + 3 * v + e) for e in range(3)]
                moved = along[0] * within + along[1] * position[1] + along[2] * position[2]
                write(1 + v, feature(3 + v) - moved)
                for e in range(3):
                    write(4 + 3 * v + e, along[e])

            terms, selectors = [], []
            for u in range(8):

                def term(q):
                    return values[group, 8 * q + u : 8 * q + u + 1, :]

                weight = weights[group, pl.ds(SLOT * u, 48, stride=ROW), :]
                heavy = [weight[8 * n : 8 * n + 8] * term(0) for n in range(6)]
                pieces = list(heavy)
                for v in range(3):
                    start = term(1 + v) + term(6 + 3 * v) * k_of
                    along = term(4 + 3 * v)
                    at = [start + term(5 + 3 * v) * j_of, start + term(5 + 3 * v) * (j_of + 2.0)]
                    for o in range(3):
                        pieces += [heavy[2 * o + h] * at[h] for h in range(2)]
                        at = [a + along for a in at]
                full = jnp.concatenate(pieces, axis=0)
                high = full.astype(jnp.bfloat16)
                low = (full - high.astype(jnp.float32)).astype(jnp.bfloat16)
                one = chosen(cells[pl.ds(8 * group + u, 1), :], 2 * BLK_DEV)
                terms += [high, low]
                selectors += [one, one]
            sums[...] += lax.dot_general(
                jnp.concatenate(terms, axis=1),
                jnp.concatenate(selectors, axis=1),
                (((1,), (1,)), ((), ())),
                preferred_element_type=jnp.float32,
            )
            return unused

        lax.fori_loop(0, CAP // 8, scatter, 0, unroll=4)

        low_half = half(16)
        for f in range(4):
            lower = [sums[48 * f + 16 * o : 48 * f + 16 * o + 16, :] for o in range(3)]
            other = [pltpu.roll(value, BLK_DEV, 1) for value in lower]
            for i in range(4):
                total = None
                if i < 3:
                    total = jnp.where(low_half, lower[i], other[i])
                if i > 0:
                    moved = jnp.where(low_half, other[i - 1], lower[i - 1])
                    total = moved if total is None else total + moved
                nodes[64 * f + 16 * i : 64 * f + 16 * i + 16, :] = total

        grid_mass = jnp.maximum(nodes[0:NODES, :], 0.5)
        node = []
        for v in range(3):
            value = nodes[(1 + v) * NODES : (2 + v) * NODES, :] / grid_mass
            if v == 2:
                value = value - STEP_DURATION * GRAVITY_ACCEL
            node.append(value * keep[...])
        if when_node is not None:
            when_node(node)
        for v in range(3):
            for o in range(3):
                value = jnp.where(low_half, node[v][16 * o : 16 * o + 16], node[v][16 * o + 16 : 16 * o + 32])
                high = value.astype(jnp.bfloat16)
                low = (value - high.astype(jnp.float32)).astype(jnp.bfloat16)
                at = 48 * v + 16 * o
                parts[at : at + 16, 0:LANES] = high
                parts[at : at + 16, LANES : 2 * LANES] = low

        def gather(group, unused):
            slots = [8 * group + u for u in range(8)]
            selectors = [chosen(cells[pl.ds(c, 1), :], 2 * BLK_DEV) for c in slots]
            selector = jnp.concatenate(selectors, axis=1)
            nodal_all = jnp.dot(
                parts[...], jnp.concatenate([selector, selector], axis=0), preferred_element_type=jnp.float32
            )
            for u, c in enumerate(slots):
                weight = weights[c // 8, pl.ds(SLOT * (c % 8), 48, stride=ROW), :]
                for v in range(3):
                    nodal = nodal_all[48 * v : 48 * (v + 1), u * LANES : (u + 1) * LANES]
                    weighted = [weight[8 * n : 8 * n + 8] * nodal[8 * n : 8 * n + 8] for n in range(6)]
                    by_i = [weighted[2 * o] + weighted[2 * o + 1] for o in range(3)]
                    odd = (weighted[1] + weighted[3]) + weighted[5]
                    outer = by_i[1] + by_i[2]
                    for t, value in enumerate((by_i[0] + outer, odd, outer + by_i[2])):
                        reduced[3 * v + t, pl.ds(ROW * c, 8, stride=SLOT), :] = value
            return unused

        lax.fori_loop(0, CAP // 8, gather, 0, unroll=2)

        def spread(v, t):
            return [reduced[3 * v + t, pl.ds(SLOT * r, CAP, stride=ROW), :] for r in range(8)]

        def add_all(terms):
            total = terms[0]
            for term in terms[1:]:
                total = total + term
            return total

        position = [rows_of(e) for e in range(3)]
        centre = [position[0] - jnp.where(position[0] >= 1.5, 1.0, 0.0), position[1], position[2]]
        alive = rows_of(15) > 0.0
        for v in range(3):
            by_row = spread(v, 0)
            by_k = [by_row[k] + by_row[4 + k] for k in range(4)]
            new_velocity = (by_k[0] + by_k[1]) + (by_k[2] + by_k[3])
            moment = [
                add_all(spread(v, 2)),
                2.0 * add_all(spread(v, 1)) + add_all(by_row[4:]),
                (by_k[1] + by_k[3]) + 2.0 * (by_k[2] + by_k[3]),
            ]
            for e in range(3):
                new_affine = 4.0 * (moment[e] - centre[e] * new_velocity)
                put(6 + 3 * v + e, jnp.where(alive, new_affine, rows_of(6 + 3 * v + e)))
            put(3 + v, jnp.where(alive, new_velocity, rows_of(3 + v)))
            new_position = jnp.clip(position[v] + STEP_DURATION * new_velocity, 0.5, 2.5)
            put(v, jnp.where(alive, new_position, position[v]))

    one_step(16)

    source = lax.broadcasted_iota(jnp.int32, (2 * MIG, LANES), 1)
    slot = lax.broadcasted_iota(jnp.int32, (2 * MIG, LANES), 0)
    for f in range(16):
        at = f * CAP + CAP - 2 * MIG
        old = state[at : at + 2 * MIG, :]
        across = jnp.where(
            source % N_CROSS == 0, pltpu.roll(old, LANES - (N_CROSS - 1), 1), pltpu.roll(old, 1, 1)
        )
        state[at : at + 2 * MIG, :] = jnp.where(slot < MIG, across, pltpu.roll(old, N_CROSS, 1))

    copy = pltpu.make_async_copy(vel, vel_hbm, sem)

    def send_velocity(node):
        lane = lax.broadcasted_iota(jnp.int32, (32, LANES), 1)
        for v in range(3):
            pairs[...] = jnp.concatenate([node[v], node[v]], axis=0).T[0:BLK_DEV, :]
            packed = jnp.where(lane < NODES, pairs[pl.ds(0, 32, stride=2), :], pairs[pl.ds(1, 32, stride=2), :])
            for q in range(32):
                vel[v : v + 1, q * LANES : (q + 1) * LANES] = packed[q : q + 1, :]
        copy.start()

    one_step(17, send_velocity)

    for j in range(BACK_ROWS):
        back_ref[pl.ds(j, DEVS, stride=BACK_ROWS), :] = state[j * LANES : (j + 1) * LANES, :].T

    copy.wait()


def in_vmem(count):
    return [pl.BlockSpec(memory_space=pltpu.VMEM)] * count


def in_hbm(count):
    return [pl.BlockSpec(memory_space=pltpu.HBM)] * count


def local(points, send_counts, block_first, block_second, contact):
    params = pltpu.CompilerParams(vmem_limit_bytes=VMEM_LIMIT)
    tiled = points.reshape(2, 8, 32, LANES).transpose(0, 2, 1, 3)
    operands = (tiled, send_counts.reshape(1, DEVS), block_first.reshape(32, LANES), block_second.reshape(32, LANES))
    send = pl.pallas_call(
        pack_kernel,
        out_shape=jax.ShapeDtypeStruct((DEVS * SEND_ROWS, LANES), jnp.float32),
        in_specs=in_hbm(4),
        out_specs=in_vmem(1)[0],
        scratch_shapes=[
            pltpu.VMEM((2, 32, 8, LANES), jnp.float32),
            pltpu.VMEM((1, DEVS), jnp.int32),
            pltpu.VMEM((32, LANES), jnp.int32),
            pltpu.VMEM((32, LANES), jnp.int32),
            pltpu.VMEM((DEVS, LANES), jnp.float32),
            pltpu.SemaphoreType.DMA((4,)),
        ],
        compiler_params=params,
    )(*(pltpu.with_memory_space_constraint(value, pltpu.HBM) for value in operands))
    got = lax.all_to_all(
        send.reshape(DEVS, 1, SEND_ROWS * LANES), ("drift", "cross"), split_axis=0, concat_axis=0, tiled=True
    )
    back, node_velocity = pl.pallas_call(
        steps_kernel,
        out_shape=(
            jax.ShapeDtypeStruct((DEVS * BACK_ROWS, LANES), jnp.float32),
            jax.ShapeDtypeStruct((3, BLK_DEV * NODES), jnp.float32),
        ),
        in_specs=in_vmem(2),
        out_specs=(in_vmem(1)[0], in_hbm(1)[0]),
        scratch_shapes=[
            pltpu.VMEM((SEND_ROWS * LANES, LANES), jnp.float32),
            pltpu.VMEM((CAP, LANES), jnp.float32),
            pltpu.VMEM((CAP // 8, 13 * 8, LANES), jnp.float32),
            pltpu.VMEM((CAP // 8, 48 * ROW, LANES), jnp.float32),
            pltpu.VMEM((192, 2 * BLK_DEV), jnp.float32),
            pltpu.VMEM((4 * NODES, LANES), jnp.float32),
            pltpu.VMEM((144, 2 * LANES), jnp.bfloat16),
            pltpu.VMEM((9, ROW * CAP, LANES), jnp.float32),
            pltpu.VMEM((NODES, LANES), jnp.float32),
            pltpu.VMEM((BLK_DEV, LANES), jnp.float32),
            pltpu.VMEM((3, BLK_DEV * NODES), jnp.float32),
            pltpu.SemaphoreType.DMA(()),
        ],
        compiler_params=params,
    )(got.reshape(DEVS * SEND_ROWS, LANES), contact.reshape(32, LANES))
    returned = lax.all_to_all(
        back.reshape(DEVS, 1, BACK_ROWS * LANES), ("drift", "cross"), split_axis=0, concat_axis=0, tiled=True
    )
    final = pl.pallas_call(
        unpack_kernel,
        out_shape=jax.ShapeDtypeStruct((2, 32, 8, LANES), jnp.float32),
        in_specs=in_vmem(1),
        out_specs=in_hbm(1)[0],
        scratch_shapes=[pltpu.VMEM((2, 32, 8, LANES), jnp.float32), pltpu.SemaphoreType.DMA((UNPACK_PARTS,))],
        compiler_params=params,
    )(returned.reshape(DEVS * BACK_ROWS, LANES))
    return (final.transpose(0, 2, 1, 3).reshape(16, DEVS * CAP), node_velocity)


def solution(mesh):
    return jax.shard_map(
        local,
        mesh=mesh,
        in_specs=(
            P(None, ("drift", "cross")),
            P(("drift", "cross")),
            P(("drift", "cross")),
            P(("drift", "cross")),
            P(("drift", "cross")),
        ),
        out_specs=(P(None, ("drift", "cross")), P(None, ("drift", "cross"))),
        check_vma=False,
    )
```

```python
import jax
import jax.numpy as jnp
from jax import lax
from jax.experimental import pallas as pl
from jax.experimental.pallas import tpu as pltpu
from jax.sharding import PartitionSpec as P

CAP = 32
MIG = 4
NODES = 64
BLK_DEV = 64
DEVS = 128
N_CROSS = 16
LANES = 128

STEP_DURATION = 0.1
GRAVITY_ACCEL = 1.0

SEND_ROWS = 5
BACK_ROWS = 4

UNPACK_PARTS = 4

ROW = 23
SLOT = 3

VMEM_LIMIT = 32 * 1024 * 1024


def spline(dist):
    size = jnp.abs(dist)
    near = 0.75 - size * size
    far = 0.5 * jnp.square(jnp.maximum(1.5 - size, 0.0))
    return jnp.where(size < 0.5, near, far)


def exchange_quarters(rows, quarter):
    turned = []
    for d in range(4):
        mixed = rows[d]
        for q in range(1, 4):
            mixed = jnp.where(quarter == q, rows[(q + d) % 4], mixed)
        turned.append(pltpu.roll(mixed, d * CAP, 1) if d else mixed)
    result = []
    for q in range(4):
        mixed = turned[-q % 4]
        for p in range(1, 4):
            mixed = jnp.where(quarter == p, turned[(p - q) % 4], mixed)
        result.append(mixed)
    return result


def pack_kernel(
    points_hbm, counts_hbm, first_hbm, second_hbm, out_ref, points_ref, counts_ref, first_ref, second_ref, counts_col, sems
):
    moves = ((counts_hbm, counts_ref), (points_hbm, points_ref), (first_hbm, first_ref), (second_hbm, second_ref))
    copies = [pltpu.make_async_copy(source, target, sems.at[n]) for n, (source, target) in enumerate(moves)]
    for copy in copies:
        copy.start()
    lane = lax.broadcasted_iota(jnp.int32, (32, LANES), 1)
    quarter = lane // CAP
    slot = (lane - 3 * CAP).astype(jnp.float32)
    copies[0].wait()
    counts = counts_ref[...].astype(jnp.float32)
    counts_col[...] = jnp.broadcast_to(counts, (DEVS, LANES)).T
    for copy in copies[1:]:
        copy.wait()

    def feature(f):
        if f < 16:
            return points_ref[f // 8, :, f % 8, :]
        return (first_ref if f == 16 else second_ref)[...].astype(jnp.float32)

    for j in range(SEND_ROWS):
        rows = [feature(4 * j + ff) if 4 * j + ff < 18 else jnp.zeros((32, LANES), jnp.float32) for ff in range(4)]
        for oo, block in enumerate(exchange_quarters(rows, quarter)):
            if j == 3:
                count = counts_col[pl.ds(oo, 32, stride=4), :]
                live = (slot < count).astype(jnp.float32)
                block = jnp.where(quarter == 3, block * live, block)
            out_ref[pl.ds(SEND_ROWS * oo + j, 32, stride=4 * SEND_ROWS), :] = block


def unpack_kernel(back_ref, out_hbm, out_ref, sems):
    tiles = 32 // UNPACK_PARTS
    lane = lax.broadcasted_iota(jnp.int32, (tiles, LANES), 1)
    quarter = lane // CAP
    copies = []
    for part in range(UNPACK_PARTS):
        at = slice(tiles * part, tiles * (part + 1))
        for j in range(BACK_ROWS):
            from_row = 4 * BACK_ROWS * tiles * part + j
            blocks = [back_ref[pl.ds(from_row + BACK_ROWS * oo, tiles, stride=4 * BACK_ROWS), :] for oo in range(4)]
            for ff, row in enumerate(exchange_quarters(blocks, quarter)):
                f = 4 * j + ff
                out_ref[f // 8, at, f % 8, :] = row
        piece = pl.ds(tiles * part, tiles)
        copies.append(pltpu.make_async_copy(out_ref.at[:, piece], out_hbm.at[:, piece], sems.at[part]))
        copies[-1].start()
    for copy in copies:
        copy.wait()


def steps_kernel(
    got_ref,
    contact_ref,
    back_ref,
    vel_hbm,
    state,
    cells,
    values,
    weights,
    sums,
    nodes,
    parts,
    reduced,
    keep,
    pairs,
    vel,
    sem,
):
    def rows_of(f):
        return state[f * CAP : (f + 1) * CAP, :]

    def put(f, value):
        state[f * CAP : (f + 1) * CAP, :] = value

    for j in range(SEND_ROWS):
        state[j * LANES : (j + 1) * LANES, :] = got_ref[pl.ds(j, DEVS, stride=SEND_ROWS), :].T

    contact = contact_ref[...]
    pairs[pl.ds(0, 32, stride=2), :] = contact
    pairs[pl.ds(1, 32, stride=2), :] = pltpu.roll(contact, NODES, 1)
    turned = jnp.concatenate([pairs[...], pairs[...]], axis=0).T
    keep[...] = 1.0 - turned[0:NODES, :]

    def half(rows):
        return lax.broadcasted_iota(jnp.int32, (rows, LANES), 1) < BLK_DEV

    def numbers(rows):
        return lax.broadcasted_iota(jnp.int32, (rows, LANES), 0).astype(jnp.float32)

    def chosen(row, rows):
        return jnp.where(numbers(rows) == row, 1.0, 0.0).astype(jnp.bfloat16)

    sub = lax.broadcasted_iota(jnp.int32, (8, LANES), 0)
    k_of = (sub % 4).astype(jnp.float32)
    j_of = (sub // 4).astype(jnp.float32)

    def one_step(ids_row, when_node=None):
        sums[...] = jnp.zeros_like(sums)

        def scatter(group, unused):
            def feature(f):
                return state[pl.ds(pl.multiple_of(f * CAP + 8 * group, 8), 8), :]

            position = [feature(e) for e in range(3)]
            mass = feature(15)
            cell = jnp.where(position[0] >= 1.5, 1.0, 0.0)
            within = position[0] - cell
            at_cells = pl.ds(pl.multiple_of(8 * group, 8), 8)
            cells[at_cells, :] = feature(ids_row) + BLK_DEV * cell
            first = [spline(within - float(o)) for o in range(3)]
            second = [spline(position[1] - float(j)) for j in range(4)]
            third = [spline(position[2] - float(k)) for k in range(4)]
            for o in range(3):
                for j in range(4):
                    product = first[o] * second[j]
                    for k in range(4):
                        r = 16 * o + 4 * j + k
                        weights[group, pl.ds(ROW * r, 8, stride=SLOT), :] = product * third[k]

            def write(q, value):
                values[group, 8 * q : 8 * q + 8, :] = value

            write(0, mass)
            for v in range(3):
                along = [feature(6 + 3 * v + e) for e in range(3)]
                moved = along[0] * within + along[1] * position[1] + along[2] * position[2]
                write(1 + v, feature(3 + v) - moved)
                for e in range(3):
                    write(4 + 3 * v + e, along[e])

            terms, selectors = [], []
            for u in range(8):

                def term(q):
                    return values[group, 8 * q + u : 8 * q + u + 1, :]

                weight = weights[group, pl.ds(SLOT * u, 48, stride=ROW), :]
                heavy = [weight[8 * n : 8 * n + 8] * term(0) for n in range(6)]
                pieces = list(heavy)
                for v in range(3):
                    start = term(1 + v) + term(6 + 3 * v) * k_of
                    along = term(4 + 3 * v)
                    at = [start + term(5 + 3 * v) * j_of, start + term(5 + 3 * v) * (j_of + 2.0)]
                    for o in range(3):
                        pieces += [heavy[2 * o + h] * at[h] for h in range(2)]
                        at = [a + along for a in at]
                full = jnp.concatenate(pieces, axis=0)
                high = full.astype(jnp.bfloat16)
                low = (full - high.astype(jnp.float32)).astype(jnp.bfloat16)
                one = chosen(cells[pl.ds(8 * group + u, 1), :], 2 * BLK_DEV)
                terms += [high, low]
                selectors += [one, one]
            sums[...] += lax.dot_general(
                jnp.concatenate(terms, axis=1),
                jnp.concatenate(selectors, axis=1),
                (((1,), (1,)), ((), ())),
                preferred_element_type=jnp.float32,
            )
            return unused

        lax.fori_loop(0, CAP // 8, scatter, 0, unroll=4)

        low_half = half(16)
        for f in range(4):
            lower = [sums[48 * f + 16 * o : 48 * f + 16 * o + 16, :] for o in range(3)]
            other = [pltpu.roll(value, BLK_DEV, 1) for value in lower]
            for i in range(4):
                total = None
                if i < 3:
                    total = jnp.where(low_half, lower[i], other[i])
                if i > 0:
                    moved = jnp.where(low_half, other[i - 1], lower[i - 1])
                    total = moved if total is None else total + moved
                nodes[64 * f + 16 * i : 64 * f + 16 * i + 16, :] = total

        grid_mass = jnp.maximum(nodes[0:NODES, :], 0.5)
        node = []
        for v in range(3):
            value = nodes[(1 + v) * NODES : (2 + v) * NODES, :] / grid_mass
            if v == 2:
                value = value - STEP_DURATION * GRAVITY_ACCEL
            node.append(value * keep[...])
        if when_node is not None:
            when_node(node)
        for v in range(3):
            for o in range(3):
                value = jnp.where(low_half, node[v][16 * o : 16 * o + 16], node[v][16 * o + 16 : 16 * o + 32])
                high = value.astype(jnp.bfloat16)
                low = (value - high.astype(jnp.float32)).astype(jnp.bfloat16)
                at = 48 * v + 16 * o
                parts[at : at + 16, 0:LANES] = high
                parts[at : at + 16, LANES : 2 * LANES] = low

        def gather(group, unused):
            slots = [8 * group + u for u in range(8)]
            selectors = [chosen(cells[pl.ds(c, 1), :], 2 * BLK_DEV) for c in slots]
            selector = jnp.concatenate(selectors, axis=1)
            nodal_all = jnp.dot(
                parts[...], jnp.concatenate([selector, selector], axis=0), preferred_element_type=jnp.float32
            )
            for u, c in enumerate(slots):
                weight = weights[c // 8, pl.ds(SLOT * (c % 8), 48, stride=ROW), :]
                for v in range(3):
                    nodal = nodal_all[48 * v : 48 * (v + 1), u * LANES : (u + 1) * LANES]
                    weighted = [weight[8 * n : 8 * n + 8] * nodal[8 * n : 8 * n + 8] for n in range(6)]
                    by_i = [weighted[2 * o] + weighted[2 * o + 1] for o in range(3)]
                    odd = (weighted[1] + weighted[3]) + weighted[5]
                    outer = by_i[1] + by_i[2]
                    for t, value in enumerate((by_i[0] + outer, odd, outer + by_i[2])):
                        reduced[3 * v + t, pl.ds(ROW * c, 8, stride=SLOT), :] = value
            return unused

        lax.fori_loop(0, CAP // 8, gather, 0, unroll=2)

        def spread(v, t):
            return [reduced[3 * v + t, pl.ds(SLOT * r, CAP, stride=ROW), :] for r in range(8)]

        def add_all(terms):
            total = terms[0]
            for term in terms[1:]:
                total = total + term
            return total

        position = [rows_of(e) for e in range(3)]
        centre = [position[0] - jnp.where(position[0] >= 1.5, 1.0, 0.0), position[1], position[2]]
        alive = rows_of(15) > 0.0
        for v in range(3):
            by_row = spread(v, 0)
            by_k = [by_row[k] + by_row[4 + k] for k in range(4)]
            new_velocity = (by_k[0] + by_k[1]) + (by_k[2] + by_k[3])
            moment = [
                add_all(spread(v, 2)),
                2.0 * add_all(spread(v, 1)) + add_all(by_row[4:]),
                (by_k[1] + by_k[3]) + 2.0 * (by_k[2] + by_k[3]),
            ]
            for e in range(3):
                new_affine = 4.0 * (moment[e] - centre[e] * new_velocity)
                put(6 + 3 * v + e, jnp.where(alive, new_affine, rows_of(6 + 3 * v + e)))
            put(3 + v, jnp.where(alive, new_velocity, rows_of(3 + v)))
            new_position = jnp.clip(position[v] + STEP_DURATION * new_velocity, 0.5, 2.5)
            put(v, jnp.where(alive, new_position, position[v]))

    one_step(16)

    source = lax.broadcasted_iota(jnp.int32, (2 * MIG, LANES), 1)
    slot = lax.broadcasted_iota(jnp.int32, (2 * MIG, LANES), 0)
    for f in range(16):
        at = f * CAP + CAP - 2 * MIG
        old = state[at : at + 2 * MIG, :]
        across = jnp.where(
            source % N_CROSS == 0, pltpu.roll(old, LANES - (N_CROSS - 1), 1), pltpu.roll(old, 1, 1)
        )
        state[at : at + 2 * MIG, :] = jnp.where(slot < MIG, across, pltpu.roll(old, N_CROSS, 1))

    copy = pltpu.make_async_copy(vel, vel_hbm, sem)

    def send_velocity(node):
        lane = lax.broadcasted_iota(jnp.int32, (32, LANES), 1)
        for v in range(3):
            pairs[...] = jnp.concatenate([node[v], node[v]], axis=0).T[0:BLK_DEV, :]
            packed = jnp.where(lane < NODES, pairs[pl.ds(0, 32, stride=2), :], pairs[pl.ds(1, 32, stride=2), :])
            for q in range(32):
                vel[v : v + 1, q * LANES : (q + 1) * LANES] = packed[q : q + 1, :]
        copy.start()

    one_step(17, send_velocity)

    for j in range(BACK_ROWS):
        back_ref[pl.ds(j, DEVS, stride=BACK_ROWS), :] = state[j * LANES : (j + 1) * LANES, :].T

    copy.wait()


def in_vmem(count):
    return [pl.BlockSpec(memory_space=pltpu.VMEM)] * count


def in_hbm(count):
    return [pl.BlockSpec(memory_space=pltpu.HBM)] * count


def local(points, send_counts, block_first, block_second, contact):
    params = pltpu.CompilerParams(vmem_limit_bytes=VMEM_LIMIT)
    tiled = points.reshape(2, 8, 32, LANES).transpose(0, 2, 1, 3)
    operands = (tiled, send_counts.reshape(1, DEVS), block_first.reshape(32, LANES), block_second.reshape(32, LANES))
    send = pl.pallas_call(
        pack_kernel,
        out_shape=jax.ShapeDtypeStruct((DEVS * SEND_ROWS, LANES), jnp.float32),
        in_specs=in_hbm(4),
        out_specs=in_vmem(1)[0],
        scratch_shapes=[
            pltpu.VMEM((2, 32, 8, LANES), jnp.float32),
            pltpu.VMEM((1, DEVS), jnp.int32),
            pltpu.VMEM((32, LANES), jnp.int32),
            pltpu.VMEM((32, LANES), jnp.int32),
            pltpu.VMEM((DEVS, LANES), jnp.float32),
            pltpu.SemaphoreType.DMA((4,)),
        ],
        compiler_params=params,
    )(*(pltpu.with_memory_space_constraint(value, pltpu.HBM) for value in operands))
    got = lax.all_to_all(
        send.reshape(DEVS, 1, SEND_ROWS * LANES), ("drift", "cross"), split_axis=0, concat_axis=0, tiled=True
    )
    back, node_velocity = pl.pallas_call(
        steps_kernel,
        out_shape=(
            jax.ShapeDtypeStruct((DEVS * BACK_ROWS, LANES), jnp.float32),
            jax.ShapeDtypeStruct((3, BLK_DEV * NODES), jnp.float32),
        ),
        in_specs=in_vmem(2),
        out_specs=(in_vmem(1)[0], in_hbm(1)[0]),
        scratch_shapes=[
            pltpu.VMEM((SEND_ROWS * LANES, LANES), jnp.float32),
            pltpu.VMEM((CAP, LANES), jnp.float32),
            pltpu.VMEM((CAP // 8, 13 * 8, LANES), jnp.float32),
            pltpu.VMEM((CAP // 8, 48 * ROW, LANES), jnp.float32),
            pltpu.VMEM((192, 2 * BLK_DEV), jnp.float32),
            pltpu.VMEM((4 * NODES, LANES), jnp.float32),
            pltpu.VMEM((144, 2 * LANES), jnp.bfloat16),
            pltpu.VMEM((9, ROW * CAP, LANES), jnp.float32),
            pltpu.VMEM((NODES, LANES), jnp.float32),
            pltpu.VMEM((BLK_DEV, LANES), jnp.float32),
            pltpu.VMEM((3, BLK_DEV * NODES), jnp.float32),
            pltpu.SemaphoreType.DMA(()),
        ],
        compiler_params=params,
    )(got.reshape(DEVS * SEND_ROWS, LANES), contact.reshape(32, LANES))
    returned = lax.all_to_all(
        back.reshape(DEVS, 1, BACK_ROWS * LANES), ("drift", "cross"), split_axis=0, concat_axis=0, tiled=True
    )
    final = pl.pallas_call(
        unpack_kernel,
        out_shape=jax.ShapeDtypeStruct((2, 32, 8, LANES), jnp.float32),
        in_specs=in_vmem(1),
        out_specs=in_hbm(1)[0],
        scratch_shapes=[pltpu.VMEM((2, 32, 8, LANES), jnp.float32), pltpu.SemaphoreType.DMA((UNPACK_PARTS,))],
        compiler_params=params,
    )(returned.reshape(DEVS * BACK_ROWS, LANES))
    return (final.transpose(0, 2, 1, 3).reshape(16, DEVS * CAP), node_velocity)


def solution(mesh):
    return jax.shard_map(
        local,
        mesh=mesh,
        in_specs=(
            P(None, ("drift", "cross")),
            P(("drift", "cross")),
            P(("drift", "cross")),
            P(("drift", "cross")),
            P(("drift", "cross")),
        ),
        out_specs=(P(None, ("drift", "cross")), P(None, ("drift", "cross"))),
        check_vma=False,
    )
```

```python
import jax
import jax.numpy as jnp
from jax import lax
from jax.experimental import pallas as pl
from jax.experimental.pallas import tpu as pltpu
from jax.sharding import PartitionSpec as P

CAP = 32
MIG = 4
NODES = 64
BLK_DEV = 64
DEVS = 128
N_CROSS = 16
LANES = 128

STEP_DURATION = 0.1
GRAVITY_ACCEL = 1.0

SEND_ROWS = 5
BACK_ROWS = 4

UNPACK_PARTS = 4

ROW = 23
SLOT = 3

VMEM_LIMIT = 32 * 1024 * 1024


def spline(dist):
    size = jnp.abs(dist)
    near = 0.75 - size * size
    far = 0.5 * jnp.square(jnp.maximum(1.5 - size, 0.0))
    return jnp.where(size < 0.5, near, far)


def exchange_quarters(rows, quarter):
    turned = []
    for d in range(4):
        mixed = rows[d]
        for q in range(1, 4):
            mixed = jnp.where(quarter == q, rows[(q + d) % 4], mixed)
        turned.append(pltpu.roll(mixed, d * CAP, 1) if d else mixed)
    result = []
    for q in range(4):
        mixed = turned[-q % 4]
        for p in range(1, 4):
            mixed = jnp.where(quarter == p, turned[(p - q) % 4], mixed)
        result.append(mixed)
    return result


def pack_kernel(
    points_hbm, counts_hbm, first_hbm, second_hbm, out_ref, points_ref, counts_ref, first_ref, second_ref, counts_col, sems
):
    moves = ((points_hbm, points_ref), (first_hbm, first_ref), (second_hbm, second_ref), (counts_hbm, counts_ref))
    copies = [pltpu.make_async_copy(source, target, sems.at[n]) for n, (source, target) in enumerate(moves)]
    for copy in copies:
        copy.start()
    lane = lax.broadcasted_iota(jnp.int32, (32, LANES), 1)
    quarter = lane // CAP
    slot = (lane - 3 * CAP).astype(jnp.float32)
    copies[3].wait()
    counts = counts_ref[...].astype(jnp.float32)
    counts_col[...] = jnp.broadcast_to(counts, (DEVS, LANES)).T
    for copy in copies[:3]:
        copy.wait()

    def feature(f):
        if f < 16:
            return points_ref[f // 8, :, f % 8, :]
        return (first_ref if f == 16 else second_ref)[...].astype(jnp.float32)

    for j in range(SEND_ROWS):
        rows = [feature(4 * j + ff) if 4 * j + ff < 18 else jnp.zeros((32, LANES), jnp.float32) for ff in range(4)]
        for oo, block in enumerate(exchange_quarters(rows, quarter)):
            if j == 3:
                count = counts_col[pl.ds(oo, 32, stride=4), :]
                live = (slot < count).astype(jnp.float32)
                block = jnp.where(quarter == 3, block * live, block)
            out_ref[pl.ds(SEND_ROWS * oo + j, 32, stride=4 * SEND_ROWS), :] = block


def unpack_kernel(back_ref, out_hbm, out_ref, sems):
    tiles = 32 // UNPACK_PARTS
    lane = lax.broadcasted_iota(jnp.int32, (tiles, LANES), 1)
    quarter = lane // CAP
    copies = []
    for part in range(UNPACK_PARTS):
        at = slice(tiles * part, tiles * (part + 1))
        for j in range(BACK_ROWS):
            from_row = 4 * BACK_ROWS * tiles * part + j
            blocks = [back_ref[pl.ds(from_row + BACK_ROWS * oo, tiles, stride=4 * BACK_ROWS), :] for oo in range(4)]
            for ff, row in enumerate(exchange_quarters(blocks, quarter)):
                f = 4 * j + ff
                out_ref[f // 8, at, f % 8, :] = row
        piece = pl.ds(tiles * part, tiles)
        copies.append(pltpu.make_async_copy(out_ref.at[:, piece], out_hbm.at[:, piece], sems.at[part]))
        copies[-1].start()
    for copy in copies:
        copy.wait()


def steps_kernel(
    got_ref,
    contact_ref,
    back_ref,
    vel_hbm,
    state,
    cells,
    values,
    weights,
    sums,
    nodes,
    parts,
    reduced,
    keep,
    pairs,
    quads,
    vel,
    sem,
):
    def rows_of(f):
        return state[f * CAP : (f + 1) * CAP, :]

    def put(f, value):
        state[f * CAP : (f + 1) * CAP, :] = value

    for j in range(SEND_ROWS):
        state[j * LANES : (j + 1) * LANES, :] = got_ref[pl.ds(j, DEVS, stride=SEND_ROWS), :].T

    contact = contact_ref[...]
    pairs[0, pl.ds(0, 32, stride=2), :] = contact
    pairs[0, pl.ds(1, 32, stride=2), :] = pltpu.roll(contact, NODES, 1)
    turned = jnp.concatenate([pairs[0], pairs[0]], axis=0).T
    keep[...] = 1.0 - turned[0:NODES, :]

    def half(rows):
        return lax.broadcasted_iota(jnp.int32, (rows, LANES), 1) < BLK_DEV

    def numbers(rows):
        return lax.broadcasted_iota(jnp.int32, (rows, LANES), 0).astype(jnp.float32)

    def chosen(row, rows):
        return jnp.where(numbers(rows) == row, 1.0, 0.0).astype(jnp.bfloat16)

    sub = lax.broadcasted_iota(jnp.int32, (8, LANES), 0)
    k_of = (sub % 4).astype(jnp.float32)
    j_of = (sub // 4).astype(jnp.float32)

    def one_step(ids_row, when_node=None):
        sums[...] = jnp.zeros_like(sums)

        def scatter(group, unused):
            def feature(f):
                return state[pl.ds(pl.multiple_of(f * CAP + 8 * group, 8), 8), :]

            position = [feature(e) for e in range(3)]
            mass = feature(15)
            cell = jnp.where(position[0] >= 1.5, 1.0, 0.0)
            within = position[0] - cell
            at_cells = pl.ds(pl.multiple_of(8 * group, 8), 8)
            cells[at_cells, :] = feature(ids_row) + BLK_DEV * cell
            first = [spline(within - float(o)) for o in range(3)]
            second = [spline(position[1] - float(j)) for j in range(4)]
            third = [spline(position[2] - float(k)) for k in range(4)]
            for o in range(3):
                for j in range(4):
                    product = first[o] * second[j]
                    for k in range(4):
                        r = 16 * o + 4 * j + k
                        weights[group, pl.ds(ROW * r, 8, stride=SLOT), :] = product * third[k]

            def write(q, value):
                values[group, 8 * q : 8 * q + 8, :] = value

            write(0, mass)
            for v in range(3):
                along = [feature(6 + 3 * v + e) for e in range(3)]
                moved = along[0] * within + along[1] * position[1] + along[2] * position[2]
                write(1 + v, feature(3 + v) - moved)
                for e in range(3):
                    write(4 + 3 * v + e, along[e])

            terms, selectors = [], []
            for u in range(8):

                def term(q):
                    return values[group, 8 * q + u : 8 * q + u + 1, :]

                weight = weights[group, pl.ds(SLOT * u, 48, stride=ROW), :]
                heavy = [weight[8 * n : 8 * n + 8] * term(0) for n in range(6)]
                pieces = list(heavy)
                for v in range(3):
                    start = term(1 + v) + term(6 + 3 * v) * k_of
                    along = term(4 + 3 * v)
                    at = [start + term(5 + 3 * v) * j_of, start + term(5 + 3 * v) * (j_of + 2.0)]
                    for o in range(3):
                        pieces += [heavy[2 * o + h] * at[h] for h in range(2)]
                        at = [a + along for a in at]
                full = jnp.concatenate(pieces, axis=0)
                high = full.astype(jnp.bfloat16)
                low = (full - high.astype(jnp.float32)).astype(jnp.bfloat16)
                one = chosen(cells[pl.ds(8 * group + u, 1), :], 2 * BLK_DEV)
                terms += [high, low]
                selectors += [one, one]
            sums[...] += lax.dot_general(
                jnp.concatenate(terms, axis=1),
                jnp.concatenate(selectors, axis=1),
                (((1,), (1,)), ((), ())),
                preferred_element_type=jnp.float32,
            )
            return unused

        lax.fori_loop(0, CAP // 8, scatter, 0, unroll=4)

        low_half = half(16)
        for f in range(4):
            lower = [sums[48 * f + 16 * o : 48 * f + 16 * o + 16, :] for o in range(3)]
            other = [pltpu.roll(value, BLK_DEV, 1) for value in lower]
            for i in range(4):
                total = None
                if i < 3:
                    total = jnp.where(low_half, lower[i], other[i])
                if i > 0:
                    moved = jnp.where(low_half, other[i - 1], lower[i - 1])
                    total = moved if total is None else total + moved
                nodes[64 * f + 16 * i : 64 * f + 16 * i + 16, :] = total

        grid_mass = jnp.maximum(nodes[0:NODES, :], 0.5)
        node = []
        for v in range(3):
            value = nodes[(1 + v) * NODES : (2 + v) * NODES, :] / grid_mass
            if v == 2:
                value = value - STEP_DURATION * GRAVITY_ACCEL
            node.append(value * keep[...])
        for v in range(3):
            for o in range(3):
                value = jnp.where(low_half, node[v][16 * o : 16 * o + 16], node[v][16 * o + 16 : 16 * o + 32])
                high = value.astype(jnp.bfloat16)
                low = (value - high.astype(jnp.float32)).astype(jnp.bfloat16)
                at = 48 * v + 16 * o
                parts[at : at + 16, 0:LANES] = high
                parts[at : at + 16, LANES : 2 * LANES] = low

        if when_node is not None:
            when_node(node)

        def gather(group, unused):
            slots = [8 * group + u for u in range(8)]
            selectors = [chosen(cells[pl.ds(c, 1), :], 2 * BLK_DEV) for c in slots]
            selector = jnp.concatenate(selectors, axis=1)
            nodal_all = jnp.dot(
                parts[...], jnp.concatenate([selector, selector], axis=0), preferred_element_type=jnp.float32
            )
            for u, c in enumerate(slots):
                weight = weights[c // 8, pl.ds(SLOT * (c % 8), 48, stride=ROW), :]
                for v in range(3):
                    nodal = nodal_all[48 * v : 48 * (v + 1), u * LANES : (u + 1) * LANES]
                    weighted = [weight[8 * n : 8 * n + 8] * nodal[8 * n : 8 * n + 8] for n in range(6)]
                    by_i = [weighted[2 * o] + weighted[2 * o + 1] for o in range(3)]
                    odd = (weighted[1] + weighted[3]) + weighted[5]
                    outer = by_i[1] + by_i[2]
                    for t, value in enumerate((by_i[0] + outer, odd, outer + by_i[2])):
                        reduced[3 * v + t, pl.ds(ROW * c, 8, stride=SLOT), :] = value
            return unused

        lax.fori_loop(0, CAP // 8, gather, 0, unroll=2)

        def spread(v, t):
            return [reduced[3 * v + t, pl.ds(SLOT * r, CAP, stride=ROW), :] for r in range(8)]

        def add_all(terms):
            total = terms[0]
            for term in terms[1:]:
                total = total + term
            return total

        position = [rows_of(e) for e in range(3)]
        centre = [position[0] - jnp.where(position[0] >= 1.5, 1.0, 0.0), position[1], position[2]]
        alive = rows_of(15) > 0.0
        for v in range(3):
            by_row = spread(v, 0)
            by_k = [by_row[k] + by_row[4 + k] for k in range(4)]
            new_velocity = (by_k[0] + by_k[1]) + (by_k[2] + by_k[3])
            moment = [
                add_all(spread(v, 2)),
                2.0 * add_all(spread(v, 1)) + add_all(by_row[4:]),
                (by_k[1] + by_k[3]) + 2.0 * (by_k[2] + by_k[3]),
            ]
            for e in range(3):
                new_affine = 4.0 * (moment[e] - centre[e] * new_velocity)
                put(6 + 3 * v + e, jnp.where(alive, new_affine, rows_of(6 + 3 * v + e)))
            put(3 + v, jnp.where(alive, new_velocity, rows_of(3 + v)))
            new_position = jnp.clip(position[v] + STEP_DURATION * new_velocity, 0.5, 2.5)
            put(v, jnp.where(alive, new_position, position[v]))

    one_step(16)

    source = lax.broadcasted_iota(jnp.int32, (2 * MIG, LANES), 1)
    slot = lax.broadcasted_iota(jnp.int32, (2 * MIG, LANES), 0)
    for f in range(16):
        at = f * CAP + CAP - 2 * MIG
        old = state[at : at + 2 * MIG, :]
        across = jnp.where(
            source % N_CROSS == 0, pltpu.roll(old, LANES - (N_CROSS - 1), 1), pltpu.roll(old, 1, 1)
        )
        state[at : at + 2 * MIG, :] = jnp.where(slot < MIG, across, pltpu.roll(old, N_CROSS, 1))

    copy = pltpu.make_async_copy(vel, vel_hbm, sem)

    def send_velocity(node):
        lane = lax.broadcasted_iota(jnp.int32, (32, LANES), 1)
        for v in range(3):
            pairs[v] = jnp.concatenate([node[v], node[v]], axis=0).T[0:BLK_DEV, :]
        for v in range(3):
            even, odd = (pairs[v, pl.ds(p, 32, stride=2), :] for p in range(2))
            packed = jnp.where(lane < NODES, even, odd)
            quads[pl.ds(v, 32, stride=4), :] = packed
        for q in range(32):
            vel[:, q * LANES : (q + 1) * LANES] = quads[4 * q : 4 * q + 3, :]
        copy.start()

    one_step(17, send_velocity)

    for j in range(BACK_ROWS):
        back_ref[pl.ds(j, DEVS, stride=BACK_ROWS), :] = state[j * LANES : (j + 1) * LANES, :].T

    copy.wait()


def in_vmem(count):
    return [pl.BlockSpec(memory_space=pltpu.VMEM)] * count


def in_hbm(count):
    return [pl.BlockSpec(memory_space=pltpu.HBM)] * count


def local(points, send_counts, block_first, block_second, contact):
    params = pltpu.CompilerParams(vmem_limit_bytes=VMEM_LIMIT)
    tiled = points.reshape(2, 8, 32, LANES).transpose(0, 2, 1, 3)
    operands = (tiled, send_counts.reshape(1, DEVS), block_first.reshape(32, LANES), block_second.reshape(32, LANES))
    send = pl.pallas_call(
        pack_kernel,
        out_shape=jax.ShapeDtypeStruct((DEVS * SEND_ROWS, LANES), jnp.float32),
        in_specs=in_hbm(4),
        out_specs=in_vmem(1)[0],
        scratch_shapes=[
            pltpu.VMEM((2, 32, 8, LANES), jnp.float32),
            pltpu.VMEM((1, DEVS), jnp.int32),
            pltpu.VMEM((32, LANES), jnp.int32),
            pltpu.VMEM((32, LANES), jnp.int32),
            pltpu.VMEM((DEVS, LANES), jnp.float32),
            pltpu.SemaphoreType.DMA((4,)),
        ],
        compiler_params=params,
    )(*(pltpu.with_memory_space_constraint(value, pltpu.HBM) for value in operands))
    got = lax.all_to_all(
        send.reshape(DEVS, 1, SEND_ROWS * LANES), ("drift", "cross"), split_axis=0, concat_axis=0, tiled=True
    )
    back, node_velocity = pl.pallas_call(
        steps_kernel,
        out_shape=(
            jax.ShapeDtypeStruct((DEVS * BACK_ROWS, LANES), jnp.float32),
            jax.ShapeDtypeStruct((3, BLK_DEV * NODES), jnp.float32),
        ),
        in_specs=in_vmem(2),
        out_specs=(in_vmem(1)[0], in_hbm(1)[0]),
        scratch_shapes=[
            pltpu.VMEM((SEND_ROWS * LANES, LANES), jnp.float32),
            pltpu.VMEM((CAP, LANES), jnp.float32),
            pltpu.VMEM((CAP // 8, 13 * 8, LANES), jnp.float32),
            pltpu.VMEM((CAP // 8, 48 * ROW, LANES), jnp.float32),
            pltpu.VMEM((192, 2 * BLK_DEV), jnp.float32),
            pltpu.VMEM((4 * NODES, LANES), jnp.float32),
            pltpu.VMEM((144, 2 * LANES), jnp.bfloat16),
            pltpu.VMEM((9, ROW * CAP, LANES), jnp.float32),
            pltpu.VMEM((NODES, LANES), jnp.float32),
            pltpu.VMEM((3, BLK_DEV, LANES), jnp.float32),
            pltpu.VMEM((LANES, LANES), jnp.float32),
            pltpu.VMEM((3, BLK_DEV * NODES), jnp.float32),
            pltpu.SemaphoreType.DMA(()),
        ],
        compiler_params=params,
    )(got.reshape(DEVS * SEND_ROWS, LANES), contact.reshape(32, LANES))
    returned = lax.all_to_all(
        back.reshape(DEVS, 1, BACK_ROWS * LANES), ("drift", "cross"), split_axis=0, concat_axis=0, tiled=True
    )
    final = pl.pallas_call(
        unpack_kernel,
        out_shape=jax.ShapeDtypeStruct((2, 32, 8, LANES), jnp.float32),
        in_specs=in_vmem(1),
        out_specs=in_hbm(1)[0],
        scratch_shapes=[pltpu.VMEM((2, 32, 8, LANES), jnp.float32), pltpu.SemaphoreType.DMA((UNPACK_PARTS,))],
        compiler_params=params,
    )(returned.reshape(DEVS * BACK_ROWS, LANES))
    return (final.transpose(0, 2, 1, 3).reshape(16, DEVS * CAP), node_velocity)


def solution(mesh):
    return jax.shard_map(
        local,
        mesh=mesh,
        in_specs=(
            P(None, ("drift", "cross")),
            P(("drift", "cross")),
            P(("drift", "cross")),
            P(("drift", "cross")),
            P(("drift", "cross")),
        ),
        out_specs=(P(None, ("drift", "cross")), P(None, ("drift", "cross"))),
        check_vma=False,
    )
```

```python
import jax
import jax.numpy as jnp
from jax import lax
from jax.experimental import pallas as pl
from jax.experimental.pallas import tpu as pltpu
from jax.sharding import PartitionSpec as P

CAP = 32
MIG = 4
NODES = 64
BLK_DEV = 64
DEVS = 128
N_CROSS = 16
LANES = 128

STEP_DURATION = 0.1
GRAVITY_ACCEL = 1.0

SEND_ROWS = 5
BACK_ROWS = 4

UNPACK_PARTS = 4

ROW = 23
SLOT = 3

VMEM_LIMIT = 32 * 1024 * 1024


def spline(dist):
    size = jnp.abs(dist)
    near = 0.75 - size * size
    far = 0.5 * jnp.square(jnp.maximum(1.5 - size, 0.0))
    return jnp.where(size < 0.5, near, far)


def exchange_quarters(rows, quarter):
    turned = []
    for d in range(4):
        mixed = rows[d]
        for q in range(1, 4):
            mixed = jnp.where(quarter == q, rows[(q + d) % 4], mixed)
        turned.append(pltpu.roll(mixed, d * CAP, 1) if d else mixed)
    result = []
    for q in range(4):
        mixed = turned[-q % 4]
        for p in range(1, 4):
            mixed = jnp.where(quarter == p, turned[(p - q) % 4], mixed)
        result.append(mixed)
    return result


def pack_kernel(
    points_hbm, counts_hbm, first_hbm, second_hbm, out_ref, points_ref, counts_ref, first_ref, second_ref, counts_col, sems
):
    moves = ((points_hbm, points_ref), (first_hbm, first_ref), (second_hbm, second_ref), (counts_hbm, counts_ref))
    copies = [pltpu.make_async_copy(source, target, sems.at[n]) for n, (source, target) in enumerate(moves)]
    for copy in copies:
        copy.start()
    lane = lax.broadcasted_iota(jnp.int32, (32, LANES), 1)
    quarter = lane // CAP
    slot = (lane - 3 * CAP).astype(jnp.float32)
    copies[3].wait()
    counts = counts_ref[...].astype(jnp.float32)
    counts_col[...] = jnp.broadcast_to(counts, (DEVS, LANES)).T
    for copy in copies[:3]:
        copy.wait()

    def feature(f):
        if f < 16:
            return points_ref[f // 8, :, f % 8, :]
        return (first_ref if f == 16 else second_ref)[...].astype(jnp.float32)

    for j in range(SEND_ROWS):
        rows = [feature(4 * j + ff) if 4 * j + ff < 18 else jnp.zeros((32, LANES), jnp.float32) for ff in range(4)]
        for oo, block in enumerate(exchange_quarters(rows, quarter)):
            if j == 3:
                count = counts_col[pl.ds(oo, 32, stride=4), :]
                live = (slot < count).astype(jnp.float32)
                block = jnp.where(quarter == 3, block * live, block)
            out_ref[pl.ds(SEND_ROWS * oo + j, 32, stride=4 * SEND_ROWS), :] = block


def unpack_kernel(back_ref, out_hbm, out_ref, sems):
    tiles = 32 // UNPACK_PARTS
    lane = lax.broadcasted_iota(jnp.int32, (tiles, LANES), 1)
    quarter = lane // CAP
    copies = []
    for part in range(UNPACK_PARTS):
        at = slice(tiles * part, tiles * (part + 1))
        for j in range(BACK_ROWS):
            from_row = 4 * BACK_ROWS * tiles * part + j
            blocks = [back_ref[pl.ds(from_row + BACK_ROWS * oo, tiles, stride=4 * BACK_ROWS), :] for oo in range(4)]
            for ff, row in enumerate(exchange_quarters(blocks, quarter)):
                f = 4 * j + ff
                out_ref[f // 8, at, f % 8, :] = row
        piece = pl.ds(tiles * part, tiles)
        copies.append(pltpu.make_async_copy(out_ref.at[:, piece], out_hbm.at[:, piece], sems.at[part]))
        copies[-1].start()
    for copy in copies:
        copy.wait()


def steps_kernel(
    got_ref,
    contact_ref,
    back_ref,
    vel_hbm,
    state,
    cells,
    values,
    weights,
    sums,
    nodes,
    parts,
    reduced,
    keep,
    pairs,
    quads,
    vel,
    sem,
):
    def rows_of(f):
        return state[f * CAP : (f + 1) * CAP, :]

    def put(f, value):
        state[f * CAP : (f + 1) * CAP, :] = value

    for j in range(SEND_ROWS):
        state[j * LANES : (j + 1) * LANES, :] = got_ref[pl.ds(j, DEVS, stride=SEND_ROWS), :].T

    contact = contact_ref[...]
    pairs[0, pl.ds(0, 32, stride=2), :] = contact
    pairs[0, pl.ds(1, 32, stride=2), :] = pltpu.roll(contact, NODES, 1)
    turned = jnp.concatenate([pairs[0], pairs[0]], axis=0).T
    keep[...] = 1.0 - turned[0:NODES, :]

    def half(rows):
        return lax.broadcasted_iota(jnp.int32, (rows, LANES), 1) < BLK_DEV

    def numbers(rows):
        return lax.broadcasted_iota(jnp.int32, (rows, LANES), 0).astype(jnp.float32)

    def chosen(row, rows):
        return jnp.where(numbers(rows) == row, 1.0, 0.0).astype(jnp.bfloat16)

    sub = lax.broadcasted_iota(jnp.int32, (8, LANES), 0)
    k_of = (sub % 4).astype(jnp.float32)
    j_of = (sub // 4).astype(jnp.float32)

    def one_step(ids_row, when_node=None):
        def scatter(group):
            def feature(f):
                return state[pl.ds(pl.multiple_of(f * CAP + 8 * group, 8), 8), :]

            position = [feature(e) for e in range(3)]
            mass = feature(15)
            cell = jnp.where(position[0] >= 1.5, 1.0, 0.0)
            within = position[0] - cell
            at_cells = pl.ds(pl.multiple_of(8 * group, 8), 8)
            cells[at_cells, :] = feature(ids_row) + BLK_DEV * cell
            first = [spline(within - float(o)) for o in range(3)]
            second = [spline(position[1] - float(j)) for j in range(4)]
            third = [spline(position[2] - float(k)) for k in range(4)]
            for o in range(3):
                for j in range(4):
                    product = first[o] * second[j]
                    for k in range(4):
                        r = 16 * o + 4 * j + k
                        weights[group, pl.ds(ROW * r, 8, stride=SLOT), :] = product * third[k]

            def write(q, value):
                values[group, 8 * q : 8 * q + 8, :] = value

            write(0, mass)
            for v in range(3):
                along = [feature(6 + 3 * v + e) for e in range(3)]
                moved = along[0] * within + along[1] * position[1] + along[2] * position[2]
                write(1 + v, feature(3 + v) - moved)
                for e in range(3):
                    write(4 + 3 * v + e, along[e])

            terms, selectors = [], []
            for u in range(8):

                def term(q):
                    return values[group, 8 * q + u : 8 * q + u + 1, :]

                weight = weights[group, pl.ds(SLOT * u, 48, stride=ROW), :]
                heavy = [weight[8 * n : 8 * n + 8] * term(0) for n in range(6)]
                pieces = list(heavy)
                for v in range(3):
                    start = term(1 + v) + term(6 + 3 * v) * k_of
                    along = term(4 + 3 * v)
                    at = [start + term(5 + 3 * v) * j_of, start + term(5 + 3 * v) * (j_of + 2.0)]
                    for o in range(3):
                        pieces += [heavy[2 * o + h] * at[h] for h in range(2)]
                        at = [a + along for a in at]
                full = jnp.concatenate(pieces, axis=0)
                high = full.astype(jnp.bfloat16)
                low = (full - high.astype(jnp.float32)).astype(jnp.bfloat16)
                one = chosen(cells[pl.ds(8 * group + u, 1), :], 2 * BLK_DEV)
                terms += [high, low]
                selectors += [one, one]
            return lax.dot_general(
                jnp.concatenate(terms, axis=1),
                jnp.concatenate(selectors, axis=1),
                (((1,), (1,)), ((), ())),
                preferred_element_type=jnp.float32,
            )

        for group in range(CAP // 8):
            part = scatter(group)
            sums[...] = part if group == 0 else sums[...] + part

        low_half = half(16)
        for f in range(4):
            lower = [sums[48 * f + 16 * o : 48 * f + 16 * o + 16, :] for o in range(3)]
            other = [pltpu.roll(value, BLK_DEV, 1) for value in lower]
            for i in range(4):
                total = None
                if i < 3:
                    total = jnp.where(low_half, lower[i], other[i])
                if i > 0:
                    moved = jnp.where(low_half, other[i - 1], lower[i - 1])
                    total = moved if total is None else total + moved
                nodes[64 * f + 16 * i : 64 * f + 16 * i + 16, :] = total

        grid_mass = jnp.maximum(nodes[0:NODES, :], 0.5)
        node = []
        for v in range(3):
            value = nodes[(1 + v) * NODES : (2 + v) * NODES, :] / grid_mass
            if v == 2:
                value = value - STEP_DURATION * GRAVITY_ACCEL
            node.append(value * keep[...])
        for v in range(3):
            for o in range(3):
                value = jnp.where(low_half, node[v][16 * o : 16 * o + 16], node[v][16 * o + 16 : 16 * o + 32])
                high = value.astype(jnp.bfloat16)
                low = (value - high.astype(jnp.float32)).astype(jnp.bfloat16)
                at = 48 * v + 16 * o
                parts[at : at + 16, 0:LANES] = high
                parts[at : at + 16, LANES : 2 * LANES] = low

        if when_node is not None:
            when_node(node)

        def gather(group, unused):
            slots = [8 * group + u for u in range(8)]
            selectors = [chosen(cells[pl.ds(c, 1), :], 2 * BLK_DEV) for c in slots]
            selector = jnp.concatenate(selectors, axis=1)
            nodal_all = jnp.dot(
                parts[...], jnp.concatenate([selector, selector], axis=0), preferred_element_type=jnp.float32
            )
            for u, c in enumerate(slots):
                weight = weights[c // 8, pl.ds(SLOT * (c % 8), 48, stride=ROW), :]
                for v in range(3):
                    nodal = nodal_all[48 * v : 48 * (v + 1), u * LANES : (u + 1) * LANES]
                    weighted = [weight[8 * n : 8 * n + 8] * nodal[8 * n : 8 * n + 8] for n in range(6)]
                    by_i = [weighted[2 * o] + weighted[2 * o + 1] for o in range(3)]
                    odd = (weighted[1] + weighted[3]) + weighted[5]
                    outer = by_i[1] + by_i[2]
                    for t, value in enumerate((by_i[0] + outer, odd, outer + by_i[2])):
                        reduced[3 * v + t, pl.ds(ROW * c, 8, stride=SLOT), :] = value
            return unused

        lax.fori_loop(0, CAP // 8, gather, 0, unroll=2)

        def spread(v, t):
            return [reduced[3 * v + t, pl.ds(SLOT * r, CAP, stride=ROW), :] for r in range(8)]

        def add_all(terms):
            total = terms[0]
            for term in terms[1:]:
                total = total + term
            return total

        position = [rows_of(e) for e in range(3)]
        centre = [position[0] - jnp.where(position[0] >= 1.5, 1.0, 0.0), position[1], position[2]]
        alive = rows_of(15) > 0.0
        for v in range(3):
            by_row = spread(v, 0)
            by_k = [by_row[k] + by_row[4 + k] for k in range(4)]
            new_velocity = (by_k[0] + by_k[1]) + (by_k[2] + by_k[3])
            moment = [
                add_all(spread(v, 2)),
                2.0 * add_all(spread(v, 1)) + add_all(by_row[4:]),
                (by_k[1] + by_k[3]) + 2.0 * (by_k[2] + by_k[3]),
            ]
            for e in range(3):
                new_affine = 4.0 * (moment[e] - centre[e] * new_velocity)
                put(6 + 3 * v + e, jnp.where(alive, new_affine, rows_of(6 + 3 * v + e)))
            put(3 + v, jnp.where(alive, new_velocity, rows_of(3 + v)))
            new_position = jnp.clip(position[v] + STEP_DURATION * new_velocity, 0.5, 2.5)
            put(v, jnp.where(alive, new_position, position[v]))

    one_step(16)

    source = lax.broadcasted_iota(jnp.int32, (2 * MIG, LANES), 1)
    slot = lax.broadcasted_iota(jnp.int32, (2 * MIG, LANES), 0)
    for f in range(16):
        at = f * CAP + CAP - 2 * MIG
        old = state[at : at + 2 * MIG, :]
        across = jnp.where(
            source % N_CROSS == 0, pltpu.roll(old, LANES - (N_CROSS - 1), 1), pltpu.roll(old, 1, 1)
        )
        state[at : at + 2 * MIG, :] = jnp.where(slot < MIG, across, pltpu.roll(old, N_CROSS, 1))

    copy = pltpu.make_async_copy(vel, vel_hbm, sem)

    def send_velocity(node):
        lane = lax.broadcasted_iota(jnp.int32, (32, LANES), 1)
        for v in range(3):
            pairs[v] = jnp.concatenate([node[v], node[v]], axis=0).T[0:BLK_DEV, :]
        for v in range(3):
            even, odd = (pairs[v, pl.ds(p, 32, stride=2), :] for p in range(2))
            packed = jnp.where(lane < NODES, even, odd)
            quads[pl.ds(v, 32, stride=4), :] = packed
        for q in range(32):
            vel[:, q * LANES : (q + 1) * LANES] = quads[4 * q : 4 * q + 3, :]
        copy.start()

    one_step(17, send_velocity)

    for j in range(BACK_ROWS):
        back_ref[pl.ds(j, DEVS, stride=BACK_ROWS), :] = state[j * LANES : (j + 1) * LANES, :].T

    copy.wait()


def in_vmem(count):
    return [pl.BlockSpec(memory_space=pltpu.VMEM)] * count


def in_hbm(count):
    return [pl.BlockSpec(memory_space=pltpu.HBM)] * count


def local(points, send_counts, block_first, block_second, contact):
    params = pltpu.CompilerParams(vmem_limit_bytes=VMEM_LIMIT)
    tiled = points.reshape(2, 8, 32, LANES).transpose(0, 2, 1, 3)
    operands = (tiled, send_counts.reshape(1, DEVS), block_first.reshape(32, LANES), block_second.reshape(32, LANES))
    send = pl.pallas_call(
        pack_kernel,
        out_shape=jax.ShapeDtypeStruct((DEVS * SEND_ROWS, LANES), jnp.float32),
        in_specs=in_hbm(4),
        out_specs=in_vmem(1)[0],
        scratch_shapes=[
            pltpu.VMEM((2, 32, 8, LANES), jnp.float32),
            pltpu.VMEM((1, DEVS), jnp.int32),
            pltpu.VMEM((32, LANES), jnp.int32),
            pltpu.VMEM((32, LANES), jnp.int32),
            pltpu.VMEM((DEVS, LANES), jnp.float32),
            pltpu.SemaphoreType.DMA((4,)),
        ],
        compiler_params=params,
    )(*(pltpu.with_memory_space_constraint(value, pltpu.HBM) for value in operands))
    got = lax.all_to_all(
        send.reshape(DEVS, 1, SEND_ROWS * LANES), ("drift", "cross"), split_axis=0, concat_axis=0, tiled=True
    )
    back, node_velocity = pl.pallas_call(
        steps_kernel,
        out_shape=(
            jax.ShapeDtypeStruct((DEVS * BACK_ROWS, LANES), jnp.float32),
            jax.ShapeDtypeStruct((3, BLK_DEV * NODES), jnp.float32),
        ),
        in_specs=in_vmem(2),
        out_specs=(in_vmem(1)[0], in_hbm(1)[0]),
        scratch_shapes=[
            pltpu.VMEM((SEND_ROWS * LANES, LANES), jnp.float32),
            pltpu.VMEM((CAP, LANES), jnp.float32),
            pltpu.VMEM((CAP // 8, 13 * 8, LANES), jnp.float32),
            pltpu.VMEM((CAP // 8, 48 * ROW, LANES), jnp.float32),
            pltpu.VMEM((192, 2 * BLK_DEV), jnp.float32),
            pltpu.VMEM((4 * NODES, LANES), jnp.float32),
            pltpu.VMEM((144, 2 * LANES), jnp.bfloat16),
            pltpu.VMEM((9, ROW * CAP, LANES), jnp.float32),
            pltpu.VMEM((NODES, LANES), jnp.float32),
            pltpu.VMEM((3, BLK_DEV, LANES), jnp.float32),
            pltpu.VMEM((LANES, LANES), jnp.float32),
            pltpu.VMEM((3, BLK_DEV * NODES), jnp.float32),
            pltpu.SemaphoreType.DMA(()),
        ],
        compiler_params=params,
    )(got.reshape(DEVS * SEND_ROWS, LANES), contact.reshape(32, LANES))
    returned = lax.all_to_all(
        back.reshape(DEVS, 1, BACK_ROWS * LANES), ("drift", "cross"), split_axis=0, concat_axis=0, tiled=True
    )
    final = pl.pallas_call(
        unpack_kernel,
        out_shape=jax.ShapeDtypeStruct((2, 32, 8, LANES), jnp.float32),
        in_specs=in_vmem(1),
        out_specs=in_hbm(1)[0],
        scratch_shapes=[pltpu.VMEM((2, 32, 8, LANES), jnp.float32), pltpu.SemaphoreType.DMA((UNPACK_PARTS,))],
        compiler_params=params,
    )(returned.reshape(DEVS * BACK_ROWS, LANES))
    return (final.transpose(0, 2, 1, 3).reshape(16, DEVS * CAP), node_velocity)


def solution(mesh):
    return jax.shard_map(
        local,
        mesh=mesh,
        in_specs=(
            P(None, ("drift", "cross")),
            P(("drift", "cross")),
            P(("drift", "cross")),
            P(("drift", "cross")),
            P(("drift", "cross")),
        ),
        out_specs=(P(None, ("drift", "cross")), P(None, ("drift", "cross"))),
        check_vma=False,
    )
```

```python
import jax
import jax.numpy as jnp
from jax import lax
from jax.experimental import pallas as pl
from jax.experimental.pallas import tpu as pltpu
from jax.sharding import PartitionSpec as P

CAP = 32
MIG = 4
NODES = 64
BLK_DEV = 64
DEVS = 128
N_CROSS = 16
LANES = 128

STEP_DURATION = 0.1
GRAVITY_ACCEL = 1.0

SEND_ROWS = 5
BACK_ROWS = 4

UNPACK_PARTS = 4

ROW = 23
SLOT = 3

VMEM_LIMIT = 32 * 1024 * 1024


def spline(dist):
    size = jnp.abs(dist)
    near = 0.75 - size * size
    far = 0.5 * jnp.square(jnp.maximum(1.5 - size, 0.0))
    return jnp.where(size < 0.5, near, far)


def exchange_quarters(rows, quarter):
    turned = []
    for d in range(4):
        mixed = rows[d]
        for q in range(1, 4):
            mixed = jnp.where(quarter == q, rows[(q + d) % 4], mixed)
        turned.append(pltpu.roll(mixed, d * CAP, 1) if d else mixed)
    result = []
    for q in range(4):
        mixed = turned[-q % 4]
        for p in range(1, 4):
            mixed = jnp.where(quarter == p, turned[(p - q) % 4], mixed)
        result.append(mixed)
    return result


def pack_kernel(
    points_hbm, counts_hbm, first_hbm, second_hbm, out_ref, points_ref, counts_ref, first_ref, second_ref, counts_col, sems
):
    moves = ((points_hbm, points_ref), (first_hbm, first_ref), (second_hbm, second_ref), (counts_hbm, counts_ref))
    copies = [pltpu.make_async_copy(source, target, sems.at[n]) for n, (source, target) in enumerate(moves)]
    for copy in copies:
        copy.start()
    lane = lax.broadcasted_iota(jnp.int32, (32, LANES), 1)
    quarter = lane // CAP
    slot = (lane - 3 * CAP).astype(jnp.float32)
    copies[3].wait()
    counts = counts_ref[...].astype(jnp.float32)
    counts_col[...] = jnp.broadcast_to(counts, (DEVS, LANES)).T
    for copy in copies[:3]:
        copy.wait()

    def feature(f):
        if f < 16:
            return points_ref[f // 8, :, f % 8, :]
        return (first_ref if f == 16 else second_ref)[...].astype(jnp.float32)

    for j in range(SEND_ROWS):
        rows = [feature(4 * j + ff) if 4 * j + ff < 18 else jnp.zeros((32, LANES), jnp.float32) for ff in range(4)]
        for oo, block in enumerate(exchange_quarters(rows, quarter)):
            if j == 3:
                count = counts_col[pl.ds(oo, 32, stride=4), :]
                live = (slot < count).astype(jnp.float32)
                block = jnp.where(quarter == 3, block * live, block)
            out_ref[pl.ds(SEND_ROWS * oo + j, 32, stride=4 * SEND_ROWS), :] = block


def unpack_kernel(back_ref, out_hbm, out_ref, sems):
    tiles = 32 // UNPACK_PARTS
    lane = lax.broadcasted_iota(jnp.int32, (tiles, LANES), 1)
    quarter = lane // CAP
    copies = []
    for part in range(UNPACK_PARTS):
        at = slice(tiles * part, tiles * (part + 1))
        for j in range(BACK_ROWS):
            from_row = 4 * BACK_ROWS * tiles * part + j
            blocks = [back_ref[pl.ds(from_row + BACK_ROWS * oo, tiles, stride=4 * BACK_ROWS), :] for oo in range(4)]
            for ff, row in enumerate(exchange_quarters(blocks, quarter)):
                f = 4 * j + ff
                out_ref[f // 8, at, f % 8, :] = row
        piece = pl.ds(tiles * part, tiles)
        copies.append(pltpu.make_async_copy(out_ref.at[:, piece], out_hbm.at[:, piece], sems.at[part]))
        copies[-1].start()
    for copy in copies:
        copy.wait()


def steps_kernel(
    got_ref,
    contact_ref,
    back_ref,
    vel_hbm,
    state,
    cells,
    values,
    weights,
    sums,
    nodes,
    parts,
    reduced,
    keep,
    pairs,
    quads,
    vel,
    sem,
):
    def rows_of(f):
        return state[f * CAP : (f + 1) * CAP, :]

    def put(f, value):
        state[f * CAP : (f + 1) * CAP, :] = value

    for j in range(SEND_ROWS):
        state[j * LANES : (j + 1) * LANES, :] = got_ref[pl.ds(j, DEVS, stride=SEND_ROWS), :].T

    contact = contact_ref[...]
    pairs[0, pl.ds(0, 32, stride=2), :] = contact
    pairs[0, pl.ds(1, 32, stride=2), :] = pltpu.roll(contact, NODES, 1)
    turned = jnp.concatenate([pairs[0], pairs[0]], axis=0).T
    keep[...] = 1.0 - turned[0:NODES, :]

    def half(rows):
        return lax.broadcasted_iota(jnp.int32, (rows, LANES), 1) < BLK_DEV

    def numbers(rows):
        return lax.broadcasted_iota(jnp.int32, (rows, LANES), 0).astype(jnp.float32)

    def chosen(row, rows):
        return jnp.where(numbers(rows) == row, 1.0, 0.0).astype(jnp.bfloat16)

    def chosen_narrow(row, rows):
        one, none = jnp.bfloat16(1.0), jnp.bfloat16(0.0)
        return jnp.where(numbers(rows).astype(jnp.bfloat16) == row.astype(jnp.bfloat16), one, none)

    sub = lax.broadcasted_iota(jnp.int32, (8, LANES), 0)
    k_of = (sub % 4).astype(jnp.float32)
    j_of = (sub // 4).astype(jnp.float32)

    def one_step(ids_row, when_node=None):
        sums[...] = jnp.zeros_like(sums)

        def scatter(group, unused):
            def feature(f):
                return state[pl.ds(pl.multiple_of(f * CAP + 8 * group, 8), 8), :]

            position = [feature(e) for e in range(3)]
            mass = feature(15)
            cell = jnp.where(position[0] >= 1.5, 1.0, 0.0)
            within = position[0] - cell
            at_cells = pl.ds(pl.multiple_of(8 * group, 8), 8)
            cells[at_cells, :] = feature(ids_row) + BLK_DEV * cell
            first = [spline(within - float(o)) for o in range(3)]
            second = [spline(position[1] - float(j)) for j in range(4)]
            third = [spline(position[2] - float(k)) for k in range(4)]
            for o in range(3):
                for j in range(4):
                    product = first[o] * second[j]
                    for k in range(4):
                        r = 16 * o + 4 * j + k
                        weights[group, pl.ds(ROW * r, 8, stride=SLOT), :] = product * third[k]

            def write(q, value):
                values[group, 8 * q : 8 * q + 8, :] = value

            write(0, mass)
            for v in range(3):
                along = [feature(6 + 3 * v + e) for e in range(3)]
                moved = along[0] * within + along[1] * position[1] + along[2] * position[2]
                write(1 + v, feature(3 + v) - moved)
                for e in range(3):
                    write(4 + 3 * v + e, along[e])

            terms, selectors = [], []
            for u in range(8):

                def term(q):
                    return values[group, 8 * q + u : 8 * q + u + 1, :]

                weight = weights[group, pl.ds(SLOT * u, 48, stride=ROW), :]
                heavy = [weight[8 * n : 8 * n + 8] * term(0) for n in range(6)]
                pieces = list(heavy)
                for v in range(3):
                    start = term(1 + v) + term(6 + 3 * v) * k_of
                    along = term(4 + 3 * v)
                    at = [start + term(5 + 3 * v) * j_of, start + term(5 + 3 * v) * (j_of + 2.0)]
                    for o in range(3):
                        pieces += [heavy[2 * o + h] * at[h] for h in range(2)]
                        at = [a + along for a in at]
                full = jnp.concatenate(pieces, axis=0)
                high = full.astype(jnp.bfloat16)
                low = (full - high.astype(jnp.float32)).astype(jnp.bfloat16)
                one = chosen(cells[pl.ds(8 * group + u, 1), :], 2 * BLK_DEV)
                terms += [high, low]
                selectors += [one, one]
            sums[...] += lax.dot_general(
                jnp.concatenate(terms, axis=1),
                jnp.concatenate(selectors, axis=1),
                (((1,), (1,)), ((), ())),
                preferred_element_type=jnp.float32,
            )
            return unused

        lax.fori_loop(0, CAP // 8, scatter, 0, unroll=4)

        low_half = half(16)
        for f in range(4):
            lower = [sums[48 * f + 16 * o : 48 * f + 16 * o + 16, :] for o in range(3)]
            other = [pltpu.roll(value, BLK_DEV, 1) for value in lower]
            for i in range(4):
                total = None
                if i < 3:
                    total = jnp.where(low_half, lower[i], other[i])
                if i > 0:
                    moved = jnp.where(low_half, other[i - 1], lower[i - 1])
                    total = moved if total is None else total + moved
                nodes[64 * f + 16 * i : 64 * f + 16 * i + 16, :] = total

        grid_mass = jnp.maximum(nodes[0:NODES, :], 0.5)
        node = []
        for v in range(3):
            value = nodes[(1 + v) * NODES : (2 + v) * NODES, :] / grid_mass
            if v == 2:
                value = value - STEP_DURATION * GRAVITY_ACCEL
            node.append(value * keep[...])
        for v in range(3):
            for o in range(3):
                value = jnp.where(low_half, node[v][16 * o : 16 * o + 16], node[v][16 * o + 16 : 16 * o + 32])
                high = value.astype(jnp.bfloat16)
                low = (value - high.astype(jnp.float32)).astype(jnp.bfloat16)
                at = 48 * v + 16 * o
                parts[at : at + 16, 0:LANES] = high
                parts[at : at + 16, LANES : 2 * LANES] = low

        if when_node is not None:
            when_node(node)

        def gather(group, unused):
            slots = [8 * group + u for u in range(8)]
            selectors = [chosen_narrow(cells[pl.ds(c, 1), :], 2 * BLK_DEV) for c in slots]
            selector = jnp.concatenate(selectors, axis=1)
            nodal_all = jnp.dot(
                parts[...], jnp.concatenate([selector, selector], axis=0), preferred_element_type=jnp.float32
            )
            for u, c in enumerate(slots):
                weight = weights[c // 8, pl.ds(SLOT * (c % 8), 48, stride=ROW), :]
                for v in range(3):
                    nodal = nodal_all[48 * v : 48 * (v + 1), u * LANES : (u + 1) * LANES]
                    weighted = [weight[8 * n : 8 * n + 8] * nodal[8 * n : 8 * n + 8] for n in range(6)]
                    by_i = [weighted[2 * o] + weighted[2 * o + 1] for o in range(3)]
                    odd = (weighted[1] + weighted[3]) + weighted[5]
                    outer = by_i[1] + by_i[2]
                    for t, value in enumerate((by_i[0] + outer, odd, outer + by_i[2])):
                        reduced[3 * v + t, pl.ds(ROW * c, 8, stride=SLOT), :] = value
            return unused

        lax.fori_loop(0, CAP // 8, gather, 0, unroll=2)

        def spread(v, t):
            return [reduced[3 * v + t, pl.ds(SLOT * r, CAP, stride=ROW), :] for r in range(8)]

        def add_all(terms):
            total = terms[0]
            for term in terms[1:]:
                total = total + term
            return total

        position = [rows_of(e) for e in range(3)]
        centre = [position[0] - jnp.where(position[0] >= 1.5, 1.0, 0.0), position[1], position[2]]
        alive = rows_of(15) > 0.0
        for v in range(3):
            by_row = spread(v, 0)
            by_k = [by_row[k] + by_row[4 + k] for k in range(4)]
            new_velocity = (by_k[0] + by_k[1]) + (by_k[2] + by_k[3])
            moment = [
                add_all(spread(v, 2)),
                2.0 * add_all(spread(v, 1)) + add_all(by_row[4:]),
                (by_k[1] + by_k[3]) + 2.0 * (by_k[2] + by_k[3]),
            ]
            for e in range(3):
                new_affine = 4.0 * (moment[e] - centre[e] * new_velocity)
                put(6 + 3 * v + e, jnp.where(alive, new_affine, rows_of(6 + 3 * v + e)))
            put(3 + v, jnp.where(alive, new_velocity, rows_of(3 + v)))
            new_position = jnp.clip(position[v] + STEP_DURATION * new_velocity, 0.5, 2.5)
            put(v, jnp.where(alive, new_position, position[v]))

    one_step(16)

    source = lax.broadcasted_iota(jnp.int32, (2 * MIG, LANES), 1)
    slot = lax.broadcasted_iota(jnp.int32, (2 * MIG, LANES), 0)
    for f in range(16):
        at = f * CAP + CAP - 2 * MIG
        old = state[at : at + 2 * MIG, :]
        across = jnp.where(
            source % N_CROSS == 0, pltpu.roll(old, LANES - (N_CROSS - 1), 1), pltpu.roll(old, 1, 1)
        )
        state[at : at + 2 * MIG, :] = jnp.where(slot < MIG, across, pltpu.roll(old, N_CROSS, 1))

    copy = pltpu.make_async_copy(vel, vel_hbm, sem)

    def send_velocity(node):
        lane = lax.broadcasted_iota(jnp.int32, (32, LANES), 1)
        for v in range(3):
            pairs[v] = jnp.concatenate([node[v], node[v]], axis=0).T[0:BLK_DEV, :]
        for v in range(3):
            even, odd = (pairs[v, pl.ds(p, 32, stride=2), :] for p in range(2))
            packed = jnp.where(lane < NODES, even, odd)
            quads[pl.ds(v, 32, stride=4), :] = packed
        for q in range(32):
            vel[:, q * LANES : (q + 1) * LANES] = quads[4 * q : 4 * q + 3, :]
        copy.start()

    one_step(17, send_velocity)

    for j in range(BACK_ROWS):
        back_ref[pl.ds(j, DEVS, stride=BACK_ROWS), :] = state[j * LANES : (j + 1) * LANES, :].T

    copy.wait()


def in_vmem(count):
    return [pl.BlockSpec(memory_space=pltpu.VMEM)] * count


def in_hbm(count):
    return [pl.BlockSpec(memory_space=pltpu.HBM)] * count


def local(points, send_counts, block_first, block_second, contact):
    params = pltpu.CompilerParams(vmem_limit_bytes=VMEM_LIMIT)
    tiled = points.reshape(2, 8, 32, LANES).transpose(0, 2, 1, 3)
    operands = (tiled, send_counts.reshape(1, DEVS), block_first.reshape(32, LANES), block_second.reshape(32, LANES))
    send = pl.pallas_call(
        pack_kernel,
        out_shape=jax.ShapeDtypeStruct((DEVS * SEND_ROWS, LANES), jnp.float32),
        in_specs=in_hbm(4),
        out_specs=in_vmem(1)[0],
        scratch_shapes=[
            pltpu.VMEM((2, 32, 8, LANES), jnp.float32),
            pltpu.VMEM((1, DEVS), jnp.int32),
            pltpu.VMEM((32, LANES), jnp.int32),
            pltpu.VMEM((32, LANES), jnp.int32),
            pltpu.VMEM((DEVS, LANES), jnp.float32),
            pltpu.SemaphoreType.DMA((4,)),
        ],
        compiler_params=params,
    )(*(pltpu.with_memory_space_constraint(value, pltpu.HBM) for value in operands))
    got = lax.all_to_all(
        send.reshape(DEVS, 1, SEND_ROWS * LANES), ("drift", "cross"), split_axis=0, concat_axis=0, tiled=True
    )
    back, node_velocity = pl.pallas_call(
        steps_kernel,
        out_shape=(
            jax.ShapeDtypeStruct((DEVS * BACK_ROWS, LANES), jnp.float32),
            jax.ShapeDtypeStruct((3, BLK_DEV * NODES), jnp.float32),
        ),
        in_specs=in_vmem(2),
        out_specs=(in_vmem(1)[0], in_hbm(1)[0]),
        scratch_shapes=[
            pltpu.VMEM((SEND_ROWS * LANES, LANES), jnp.float32),
            pltpu.VMEM((CAP, LANES), jnp.float32),
            pltpu.VMEM((CAP // 8, 13 * 8, LANES), jnp.float32),
            pltpu.VMEM((CAP // 8, 48 * ROW, LANES), jnp.float32),
            pltpu.VMEM((192, 2 * BLK_DEV), jnp.float32),
            pltpu.VMEM((4 * NODES, LANES), jnp.float32),
            pltpu.VMEM((144, 2 * LANES), jnp.bfloat16),
            pltpu.VMEM((9, ROW * CAP, LANES), jnp.float32),
            pltpu.VMEM((NODES, LANES), jnp.float32),
            pltpu.VMEM((3, BLK_DEV, LANES), jnp.float32),
            pltpu.VMEM((LANES, LANES), jnp.float32),
            pltpu.VMEM((3, BLK_DEV * NODES), jnp.float32),
            pltpu.SemaphoreType.DMA(()),
        ],
        compiler_params=params,
    )(got.reshape(DEVS * SEND_ROWS, LANES), contact.reshape(32, LANES))
    returned = lax.all_to_all(
        back.reshape(DEVS, 1, BACK_ROWS * LANES), ("drift", "cross"), split_axis=0, concat_axis=0, tiled=True
    )
    final = pl.pallas_call(
        unpack_kernel,
        out_shape=jax.ShapeDtypeStruct((2, 32, 8, LANES), jnp.float32),
        in_specs=in_vmem(1),
        out_specs=in_hbm(1)[0],
        scratch_shapes=[pltpu.VMEM((2, 32, 8, LANES), jnp.float32), pltpu.SemaphoreType.DMA((UNPACK_PARTS,))],
        compiler_params=params,
    )(returned.reshape(DEVS * BACK_ROWS, LANES))
    return (final.transpose(0, 2, 1, 3).reshape(16, DEVS * CAP), node_velocity)


def solution(mesh):
    return jax.shard_map(
        local,
        mesh=mesh,
        in_specs=(
            P(None, ("drift", "cross")),
            P(("drift", "cross")),
            P(("drift", "cross")),
            P(("drift", "cross")),
            P(("drift", "cross")),
        ),
        out_specs=(P(None, ("drift", "cross")), P(None, ("drift", "cross"))),
        check_vma=False,
    )
```
